32 devices in a mesh: ens: 1, lon: 16 (over z, y, x), lat: 2 (over core).
Axes of the slice: x: 2, y: 2, z: 4, core: 2. Of those that a mesh axis runs over, the one named last changes fastest.
Arguments:
- fields: bfloat16 [128, 64, 1024], P('lat', 'lon'), may hold values from -6 to 6
- land_mask: int32 [128, 64], P('lat', 'lon'), may hold values 0 or 1
- land_embed: float32 [1024], replicated, may hold values from -3 to 3
- column_gain: float32 [1024], replicated, may hold values from 0.1 to 1.9
- row_gain: float32 [1024], replicated, may hold values from 0.1 to 1.9
- column_slopes: float32 [8], replicated, may hold values from 0.02 to 0.3
- row_slopes: float32 [8], replicated, may hold values from 0.02 to 0.3
- column_project: bfloat16 [1024, 1536], P('lon', 'lat'), may hold values from -0.1875 to 0.1875
- column_output: bfloat16 [1024, 512], P('lon', 'lat'), may hold values from -0.5 to 0.5
- row_project: bfloat16 [1024, 1536], P('lon', 'lat'), may hold values from -0.1875 to 0.1875
- row_output: bfloat16 [1024, 512], P('lon', 'lat'), may hold values from -0.5 to 0.5
Outputs:
- block_output: bfloat16 [128, 64, 1024], P(('ens', 'lat'), 'lon')
The draws below stay inside these ranges and needn't reach their ends.
All inputs are finite; a program needn't handle non-finite values. No bound on the sum of `land_mask` on one device may be relied on, other than what follows from the above.
Results may differ from the reference program's by a relative error of at most 0.012.
Values may be sent and summed in bfloat16 or wider, within the bound.
No kernel may reach another device: no remote copies, remote signals or barrier semaphores. Data moves between devices by JAX's collectives and lax.ppermute only.
A program may use at most 64 MiB of HBM per device.

```python
import math
import jax
import jax.numpy as jnp
from jax import lax

D = 1024
HEADS = 8
HS = 64
H = 128
W = 64
HD = 512


def plant(values, stream_key, smallest, largest):
    spot = [jax.random.randint(jax.random.fold_in(stream_key, axis), (), 0, length) for axis, length in enumerate(values.shape)]
    widest = values.shape.index(max(values.shape))
    next_to = spot[:widest] + [(spot[widest] + 1) % values.shape[widest]] + spot[widest + 1:]
    return values.at[tuple(spot)].set(smallest).at[tuple(next_to)].set(largest)


def shard_levels(own_key, shape, cuts, least, top_value):
    factor_of = 1.0
    for position, parts in cuts:
        steps = jax.random.uniform(jax.random.fold_in(jax.random.fold_in(own_key, 6), position), (parts,), jnp.float32, least / len(cuts), top_value / len(cuts))
        factor_of = factor_of * jnp.repeat(jnp.exp(steps), shape[position] // parts).reshape((-1,) + (1,) * (len(shape) - 1 - position))
    return factor_of


def noise(own_key, shape, scale, bound, cuts=(), kind=jnp.bfloat16):
    loudness = shard_levels(own_key, shape, cuts, -0.22, 0.18) if cuts else 1.0
    drawn = jax.random.normal(own_key, shape, jnp.float32) * scale * loudness
    return jnp.minimum(jnp.maximum(drawn, -bound), bound).astype(kind)


def setup_inputs(seed: int = 0, part: int = 0) -> dict:
    splits = jax.random.split(jax.random.key(seed), 12)
    fields = noise(splits[0], (H, W, D), 1.0, 6.0, ((0, 2), (1, 16)))
    land_mask = plant((jax.random.randint(splits[1], (H, W), 0, 3) < 1).astype(jnp.int32), jax.random.fold_in(splits[1], 1), 0, 1)
    land_embed = noise(splits[2], (D,), 0.5, 3.0, (), jnp.float32)
    column_gain = jnp.clip(1.0 + 0.18 * jax.random.normal(splits[3], (D,), jnp.float32), 0.1, 1.9)
    row_gain = jnp.clip(1.0 + 0.18 * jax.random.normal(splits[4], (D,), jnp.float32), 0.1, 1.9)
    column_slopes = jnp.clip(jnp.exp(jax.random.uniform(splits[5], (HEADS,), jnp.float32, math.log(0.02), math.log(0.3))), 0.02, 0.3)
    row_slopes = jnp.clip(jnp.exp(jax.random.uniform(splits[6], (HEADS,), jnp.float32, math.log(0.02), math.log(0.3))), 0.02, 0.3)
    column_project = noise(splits[7], (D, 3 * HD), D ** -0.5, 0.1875, ((0, 16), (1, 2)))
    column_output = noise(splits[8], (D, HD), (HD // 4) ** -0.5, 0.5, ((0, 16), (1, 2)))
    row_project = noise(splits[9], (D, 3 * HD), D ** -0.5, 0.1875, ((0, 16), (1, 2)))
    row_output = noise(splits[10], (D, HD), (HD // 4) ** -0.5, 0.5, ((0, 16), (1, 2)))
    return dict(fields=fields, land_mask=land_mask, land_embed=land_embed, column_gain=column_gain, row_gain=row_gain, column_slopes=column_slopes, row_slopes=row_slopes, column_project=column_project, column_output=column_output, row_project=row_project, row_output=row_output)


def layer_norm(values, gain):
    center = values - lax.optimization_barrier(jnp.mean(values, axis=-1, keepdims=True))
    spread = lax.optimization_barrier(jnp.mean(center * center, axis=-1, keepdims=True))
    return center * lax.rsqrt(spread + 1e-05) * gain

def unit_rms(vectors):
    return vectors * lax.rsqrt(lax.optimization_barrier(jnp.mean(vectors * vectors, axis=-1, keepdims=True)) + 1e-06)

def heads_of(projected):
    query = unit_rms(projected[..., 0, :]).astype(jnp.bfloat16)
    keyed = unit_rms(projected[..., 1, :]).astype(jnp.bfloat16)
    valued = projected[..., 2, :].astype(jnp.bfloat16)
    return lax.optimization_barrier((query, keyed, valued))

def head_first(array):
    return jnp.moveaxis(array, 2, 0).astype(jnp.float32)

def reference(fields, land_mask, land_embed, column_gain, row_gain, column_slopes, row_slopes, column_project, column_output, row_project, row_output):
    lat_rows, lon_cols, width = fields.shape
    scale = 1.0 / math.sqrt(HS)
    start = fields.astype(jnp.float32) + land_mask.astype(jnp.float32)[..., None] * land_embed
    normed = layer_norm(start, column_gain).astype(jnp.bfloat16)
    projected = jnp.dot(normed.reshape(-1, width), column_project, preferred_element_type=jnp.float32)
    query, keyed, valued = heads_of(projected.reshape(lat_rows, lon_cols, HEADS, 3, HS))
    far_keys = jnp.roll(keyed, lon_cols // 2, axis=1)
    far_values = jnp.roll(valued, lon_cols // 2, axis=1)
    rows_here = jnp.arange(lat_rows, dtype=jnp.int32)
    near_dist = jnp.abs(rows_here[:, None] - rows_here[None, :]).astype(jnp.float32)
    pair_sum = rows_here[:, None] + rows_here[None, :]
    far_dist = jnp.minimum(pair_sum + 1, 2 * lat_rows - 1 - pair_sum).astype(jnp.float32)

    def column_head(pieces):
        query_h, key_h, value_h, far_key_h, far_value_h, slope = pieces
        near_score = jnp.einsum('rcd,scd->crs', query_h, key_h) * scale - slope * near_dist
        far_score = jnp.einsum('rcd,scd->crs', query_h, far_key_h) * scale - slope * far_dist
        near_weight = jnp.exp(near_score)
        far_weight = jnp.exp(far_score)
        total = lax.optimization_barrier(jnp.sum(near_weight, axis=-1, keepdims=True)) + lax.optimization_barrier(jnp.sum(far_weight, axis=-1, keepdims=True))
        near_prob = lax.optimization_barrier((near_weight / total).astype(jnp.bfloat16)).astype(jnp.float32)
        far_prob = lax.optimization_barrier((far_weight / total).astype(jnp.bfloat16)).astype(jnp.float32)
        mixed = jnp.einsum('crs,scd->rcd', near_prob, value_h) + jnp.einsum('crs,scd->rcd', far_prob, far_value_h)
        return mixed.astype(jnp.bfloat16)
    column_mixed = lax.map(column_head, (head_first(query), head_first(keyed), head_first(valued), head_first(far_keys), head_first(far_values), column_slopes.astype(jnp.float32)))
    column_mixed = jnp.moveaxis(column_mixed, 0, 2).reshape(lat_rows * lon_cols, HEADS * HS)
    update = jnp.dot(column_mixed, column_output.T, preferred_element_type=jnp.float32)
    middle = start + update.reshape(lat_rows, lon_cols, width)
    row_normed = layer_norm(middle, row_gain).astype(jnp.bfloat16)
    projected = jnp.dot(row_normed.reshape(-1, width), row_project, preferred_element_type=jnp.float32)
    query, keyed, valued = heads_of(projected.reshape(lat_rows, lon_cols, HEADS, 3, HS))
    cols_here = jnp.arange(lon_cols, dtype=jnp.int32)
    gap = jnp.abs(cols_here[:, None] - cols_here[None, :])
    cycle_dist = jnp.minimum(gap, lon_cols - gap).astype(jnp.float32)

    def row_head(pieces):
        query_h, key_h, value_h, slope = pieces
        score = jnp.einsum('rcd,red->rce', query_h, key_h) * scale - slope * cycle_dist
        weight = jnp.exp(score)
        prob = weight / lax.optimization_barrier(jnp.sum(weight, axis=-1, keepdims=True))
        prob = lax.optimization_barrier(prob.astype(jnp.bfloat16)).astype(jnp.float32)
        return jnp.einsum('rce,red->rcd', prob, value_h).astype(jnp.bfloat16)
    row_mixed = lax.map(row_head, (head_first(query), head_first(keyed), head_first(valued), row_slopes.astype(jnp.float32)))
    row_mixed = jnp.moveaxis(row_mixed, 0, 2).reshape(lat_rows * lon_cols, HEADS * HS)
    update = jnp.dot(row_mixed, row_output.T, preferred_element_type=jnp.float32)
    return (middle + update.reshape(lat_rows, lon_cols, width)).astype(jnp.bfloat16)
```

```python
import functools
import math

import jax
import jax.numpy as jnp
from jax import lax
from jax.experimental import pallas as pl
from jax.experimental.pallas import tpu as pltpu
from jax.sharding import PartitionSpec as P

HS = 64
PAIR = 2 * HS
PLANE = 4
NEVER = -1e30


def at(place, length):
    return [(i, place(i)) for i in range(length)]


def swap_bands(value):
    return lax.ppermute(value, "lat", at(lambda i: 1 - i, 2))


def whole(shape, index=None):
    return pl.BlockSpec(shape, lambda _: index or (0,) * len(shape))


SCALARS = pl.BlockSpec(memory_space=pltpu.SMEM)


def call(kernel, out, name, in_specs, scratch=(), cost=1e9):
    return pl.pallas_call(
        kernel,
        grid=(1,),
        out_shape=out,
        in_specs=in_specs,
        out_specs=jax.tree.map(lambda o: whole(o.shape), out),
        scratch_shapes=scratch,
        compiler_params=pltpu.CompilerParams(vmem_limit_bytes=40 * 2**20),
        cost_estimate=pl.CostEstimate(flops=int(cost), bytes_accessed=4 * 2**20, transcendentals=2**19),
        name=name,
    )


def dot(a, b):
    return jnp.dot(a, b, preferred_element_type=jnp.float32)


def dot_t(a, b):
    return lax.dot_general(a, b, (((1,), (1,)), ((), ())), preferred_element_type=jnp.float32)


def iota(shape, axis):
    return lax.broadcasted_iota(jnp.int32, shape, axis)


def by_kind(weight):
    rows, cols = weight.shape
    heads = cols // (3 * HS)
    return weight.reshape(rows, heads, 3, HS).transpose(0, 2, 1, 3).reshape(rows, cols)


def along_lines(weight, length):
    lines = length // PLANE
    parts = [weight]
    for k in range(1, lines):
        parts.append(lax.ppermute(weight, "lon", at(lambda i: (i + PLANE * k) % length, length)))
    return jnp.concatenate(parts, axis=0)


def across_plane(part, length):
    return [part] + [lax.ppermute(part, "lon", at(lambda i: i ^ k, length)) for k in range(1, PLANE)]


def put_in_order(target, pieces, place, rows):
    lines = pieces[0].shape[0] // rows
    line, spot = place[0] // PLANE, place[0] % PLANE
    for j, piece in enumerate(pieces):
        for k in range(lines):
            owner = lax.rem(line - k + lines, lines) * PLANE + lax.bitwise_xor(spot, j)
            target[pl.ds(pl.multiple_of(owner * rows, rows), rows), :] = piece[
                k * rows : (k + 1) * rows, :
            ]


def norm(values, gain):
    center = values - jnp.mean(values, axis=-1, keepdims=True)
    spread = jnp.mean(center * center, axis=-1, keepdims=True)
    return center * lax.rsqrt(spread + 1e-05) * gain


def land_start(tokens_ref, mask_ref, embed_ref):
    rows, cols = mask_ref.shape
    total = rows * cols
    row_of = (iota((total, rows), 0) // cols == iota((total, rows), 1)).astype(jnp.bfloat16)
    spread = dot(row_of, mask_ref[...].astype(jnp.bfloat16))
    own = iota((total, cols), 0) % cols == iota((total, cols), 1)
    land = jnp.sum(jnp.where(own, spread, 0.0), axis=1, keepdims=True)
    return tokens_ref[...].astype(jnp.float32) + land * embed_ref[...]


def reorder(total, minor):
    major = total // minor
    d, t = iota((total, total), 0), iota((total, total), 1)
    return (t == (d % major) * minor + d // major).astype(jnp.bfloat16)


def start_kernel(tokens_ref, mask_ref, embed_ref, gain_ref, out_ref):
    start = land_start(tokens_ref, mask_ref, embed_ref)
    normed = norm(start, gain_ref[...]).astype(jnp.bfloat16)
    cols = mask_ref.shape[1]
    out_ref[...] = dot(reorder(normed.shape[0], cols), normed).astype(jnp.bfloat16)


def unit_heads(vectors, scale=1.0):
    width = vectors.shape[1]
    same = (iota((width, width), 0) // HS == iota((width, width), 1) // HS).astype(jnp.bfloat16)
    total = dot((vectors * vectors).astype(jnp.bfloat16), same)
    return (vectors * (lax.rsqrt(total * (1.0 / HS) + 1e-06) * scale)).astype(jnp.bfloat16)


def two_heads(query, keyed, valued, bias):
    rows = query.shape[0]
    first = iota(query.shape, 1) < HS
    zero = jnp.zeros_like(query)
    stacked = jnp.concatenate([jnp.where(first, query, zero), jnp.where(first, zero, query)], axis=0)
    weight = jnp.exp(dot_t(stacked, keyed) + bias).astype(jnp.bfloat16)
    widened = jnp.concatenate([valued, jnp.ones_like(valued)], axis=1)
    mixed = dot(weight, widened)
    mixed = mixed[:, :PAIR] / mixed[:, PAIR:]
    return jnp.where(first, mixed[:rows], mixed[rows:]).astype(jnp.bfloat16)


def column_kernel(
    shard, cols, place, slopes, own, other, far_own, far_other, w0, w1, w2, w3, out_own, out_other, weight, qkv, far
):
    put_in_order(weight, (w0, w1, w2, w3), place, shard)
    tokens = own.shape[0]
    band = tokens // cols
    width = weight.shape[1] // 3
    for half, ref in enumerate((own, other)):
        at_rows = slice(half * tokens, (half + 1) * tokens)
        projected = dot(ref[...], weight[...])
        qkv[at_rows, :width] = unit_heads(projected[:, :width], 1.0 / math.sqrt(HS))
        qkv[at_rows, width : 2 * width] = unit_heads(projected[:, width : 2 * width])
        qkv[at_rows, 2 * width :] = projected[:, 2 * width :].astype(jnp.bfloat16)
    for half, ref in enumerate((far_own, far_other)):
        at_rows = slice(half * tokens, (half + 1) * tokens)
        projected = dot(ref[...], weight[:, width:])
        far[at_rows, :width] = unit_heads(projected[:, :width])
        far[at_rows, width:] = projected[:, width:].astype(jnp.bfloat16)
    total = 2 * band
    lat = place[1]
    shape = (total, 2 * total)
    spot_q, spot_k = iota(shape, 0), iota(shape, 1)
    shift = lat * band
    row_q = (spot_q + shift) % total
    row_k = (spot_k % total + shift) % total
    near = jnp.abs(row_q - row_k)
    pair_sum = row_q + row_k
    beyond = jnp.minimum(pair_sum + 1, 2 * total - 1 - pair_sum)
    distance = jnp.where(spot_k < total, near, beyond).astype(jnp.float32)
    mixed_own, mixed_other = [], []
    for pair in range(width // PAIR):
        bias = jnp.concatenate(
            [distance * -slopes[2 * pair], distance * -slopes[2 * pair + 1]], axis=0
        )
        lanes = lambda kind: slice(kind * width + pair * PAIR, kind * width + (pair + 1) * PAIR)
        got_own, got_other = [], []
        for c in range(cols):
            here = slice(c * band, (c + 1) * band)
            there = slice(tokens + c * band, tokens + (c + 1) * band)
            both = lambda ref, kind: [ref[here, lanes(kind)], ref[there, lanes(kind)]]
            query = jnp.concatenate(both(qkv, 0), axis=0)
            keyed = jnp.concatenate(both(qkv, 1) + both(far, 0), axis=0)
            valued = jnp.concatenate(both(qkv, 2) + both(far, 1), axis=0)
            mixed = two_heads(query, keyed, valued, bias)
            got_own.append(mixed[:band])
            got_other.append(mixed[band:])
        mixed_own.append(jnp.concatenate(got_own, axis=0))
        mixed_other.append(jnp.concatenate(got_other, axis=0))
    back = reorder(tokens, band)
    out_own[...] = dot(back, jnp.concatenate(mixed_own, axis=1)).astype(jnp.bfloat16)
    out_other[...] = dot(back, jnp.concatenate(mixed_other, axis=1)).astype(jnp.bfloat16)


def middle_kernel(
    shard, place, tokens, mask, embed, gain, mine, theirs, w0, w1, w2, w3, u0, u1, u2, u3, middle, out, near, far
):
    put_in_order(near, (w0, w1, w2, w3), place, shard)
    put_in_order(far, (u0, u1, u2, u3), place, shard)
    update = dot_t(mine[...], near[...]) + dot_t(theirs[...], far[...])
    value = land_start(tokens, mask, embed) + update
    middle[...] = value
    out[...] = norm(value, gain[...]).astype(jnp.bfloat16)


def row_kernel(shard, cols, rows, place, slopes, tokens, w0, w1, w2, w3, u0, u1, u2, u3, out, near, far):
    put_in_order(near, (w0, w1, w2, w3), place, shard)
    put_in_order(far, (u0, u1, u2, u3), place, shard)
    total = tokens.shape[0]
    block = cols * rows
    lon_count = total // block
    circle = lon_count * cols
    spot_q, spot_k = iota((total, total), 0), iota((total, total), 1)
    lon_of = lambda spot: spot // block * cols + spot % cols
    row_of = lambda spot: spot % block // cols
    gap = jnp.abs(lon_of(spot_q) - lon_of(spot_k))
    distance = jnp.minimum(gap, circle - gap).astype(jnp.float32)
    same = row_of(spot_q) == row_of(spot_k)
    width = near.shape[1] // 3
    heads = width // HS
    for half, ref in enumerate((near, far)):
        projected = dot(tokens[...], ref[...])
        query = unit_heads(projected[:, :width], 1.0 / math.sqrt(HS))
        keyed = unit_heads(projected[:, width : 2 * width])
        valued = projected[:, 2 * width :].astype(jnp.bfloat16)
        for pair in range(width // PAIR):
            lanes = slice(pair * PAIR, (pair + 1) * PAIR)
            bias = jnp.concatenate(
                [
                    jnp.where(same, distance * -slopes[half * heads + 2 * pair + one], NEVER)
                    for one in range(2)
                ],
                axis=0,
            )
            mixed = two_heads(query[:, lanes], keyed[:, lanes], valued[:, lanes], bias)
            start = half * width + pair * PAIR
            out[:, start : start + PAIR] = mixed


def final_kernel(shard, place, middle, mixed, w0, w1, w2, w3, u0, u1, u2, u3, out, near, far):
    put_in_order(near, (w0, w1, w2, w3), place, shard)
    put_in_order(far, (u0, u1, u2, u3), place, shard)
    width = near.shape[1]
    update = dot_t(mixed[:, :width], near[...]) + dot_t(mixed[:, width:], far[...])
    out[...] = (middle[...] + update).astype(jnp.bfloat16)


def fast(
    fields,
    land_mask,
    land_embed,
    column_gain,
    row_gain,
    column_slopes,
    row_slopes,
    column_project,
    column_output,
    row_project,
    row_output,
):
    lon_count = lax.axis_size("lon")
    lat = lax.axis_index("lat")
    lon = lax.axis_index("lon")
    band, cols, width = fields.shape
    tokens = band * cols
    heads = column_slopes.shape[0]
    half = heads // 2
    attend = half * HS
    shard = column_project.shape[0]
    place = jnp.stack([lon, lat]).astype(jnp.int32)
    embed, column_gain, row_gain = (v.reshape(1, width) for v in (land_embed, column_gain, row_gain))
    own_slopes = lax.dynamic_slice_in_dim(column_slopes, lat * half, half)
    turned = jnp.roll(row_slopes, -lat * half)

    first = along_lines(by_kind(column_project), lon_count)
    flat = fields.reshape(tokens, width)
    bf16 = lambda *shape: jax.ShapeDtypeStruct(shape, jnp.bfloat16)
    f32 = lambda *shape: jax.ShapeDtypeStruct(shape, jnp.float32)
    token_block = whole((tokens, width))
    mask_block = whole((band, cols))
    row_block = whole((1, width))
    normed = call(
        start_kernel,
        bf16(tokens, width),
        "column_normed",
        [token_block, mask_block, row_block, row_block],
    )(flat, land_mask, embed, column_gain)
    other = swap_bands(normed)
    far_own = lax.ppermute(normed, "lon", at(lambda i: (i + lon_count // 2) % lon_count, lon_count))
    pieces = across_plane(first, lon_count)
    far_other = swap_bands(far_own)

    rest = jnp.concatenate([by_kind(row_project), column_output, row_output], axis=1)
    rest = along_lines(rest, lon_count)
    rest_near = across_plane(rest, lon_count)
    rest_far = [swap_bands(piece) for piece in rest_near]

    part = rest.shape[0]
    project_specs = [whole((part, 3 * attend))] * PLANE
    column_out_specs = [whole((part, attend), (0, 3))] * PLANE
    row_out_specs = [whole((part, attend), (0, 4))] * PLANE
    wide = pltpu.VMEM((shard * lon_count, 3 * attend), jnp.bfloat16)
    narrow = pltpu.VMEM((shard * lon_count, attend), jnp.bfloat16)

    mixed_own, mixed_other = call(
        functools.partial(column_kernel, shard, cols),
        (bf16(tokens, attend), bf16(tokens, attend)),
        "column_attention",
        [SCALARS, SCALARS] + [token_block] * 4 + project_specs,
        [
            wide,
            pltpu.VMEM((2 * tokens, 3 * attend), jnp.bfloat16),
            pltpu.VMEM((2 * tokens, 2 * attend), jnp.bfloat16),
        ],
    )(place, own_slopes, normed, other, far_own, far_other, *pieces)
    theirs = swap_bands(mixed_other)
    mixed_block = whole((tokens, attend))
    middle, row_normed = call(
        functools.partial(middle_kernel, shard),
        (f32(tokens, width), bf16(tokens, width)),
        "middle",
        [SCALARS, token_block, mask_block, row_block, row_block, mixed_block, mixed_block]
        + column_out_specs * 2,
        [narrow, narrow],
    )(place, flat, land_mask, embed, row_gain, mixed_own, theirs, *rest_near, *rest_far)
    spread = lax.all_to_all(row_normed, "lon", split_axis=0, concat_axis=0, tiled=True)
    row_mixed = call(
        functools.partial(row_kernel, shard, cols, band // lon_count),
        bf16(tokens, 2 * attend),
        "row_attention",
        [SCALARS, SCALARS, token_block] + project_specs * 2,
        [wide, wide],
    )(place, turned, spread, *rest_near, *rest_far)
    back = lax.all_to_all(row_mixed, "lon", split_axis=0, concat_axis=0, tiled=True)
    out = call(
        functools.partial(final_kernel, shard),
        bf16(tokens, width),
        "block_output",
        [SCALARS, token_block, whole((tokens, 2 * attend))] + row_out_specs * 2,
        [narrow, narrow],
    )(place, middle, back, *rest_near, *rest_far)
    return out.reshape(band, cols, width)


def passed_along(value, axis, by):
    length = lax.axis_size(axis)
    return lax.ppermute(value, axis, [(i, (i + by) % length) for i in range(length)])


def layer_norm(values, gain):
    center = values - jnp.mean(values, axis=-1, keepdims=True)
    spread = jnp.mean(center * center, axis=-1, keepdims=True)
    return center * lax.rsqrt(spread + 1e-05) * gain


def unit_rms(vectors):
    return vectors * lax.rsqrt(jnp.mean(vectors * vectors, axis=-1, keepdims=True) + 1e-06)


def head_split(projected):
    query = unit_rms(projected[..., 0, :]).astype(jnp.bfloat16)
    keyed = unit_rms(projected[..., 1, :]).astype(jnp.bfloat16)
    valued = projected[..., 2, :].astype(jnp.bfloat16)
    return (query, keyed, valued)


def gather_bands(normed):
    return lax.all_gather(normed, "lat", axis=0, tiled=True)


def sum_heads(partial_value):
    return lax.psum_scatter(
        partial_value.astype(jnp.bfloat16), "lat", scatter_dimension=0, tiled=True
    ).astype(jnp.float32)


def project_in(normed, weight):
    return jnp.dot(
        normed,
        lax.all_gather(weight, "lon", axis=0, tiled=True),
        preferred_element_type=jnp.float32,
    )


def project_out(mixed, weight):
    return lax.dot_general(
        mixed,
        lax.all_gather(weight, "lon", axis=0, tiled=True),
        (((1,), (1,)), ((), ())),
        preferred_element_type=jnp.float32,
    )


def column_attend(query, column_kv, far_kv, slopes):
    total_rows = column_kv.shape[0]
    keyed = jnp.concatenate([column_kv[..., :HS], far_kv[..., :HS]], axis=0)
    valued = jnp.concatenate([column_kv[..., HS:], far_kv[..., HS:]], axis=0)
    scores = jnp.einsum("rchd,schd->chrs", query, keyed, preferred_element_type=jnp.float32)
    rows_here = jnp.arange(query.shape[0], dtype=jnp.int32)
    key_rows = jnp.arange(total_rows, dtype=jnp.int32)
    near_dist = jnp.abs(rows_here[:, None] - key_rows[None, :])
    pair_sum = rows_here[:, None] + key_rows[None, :]
    far_dist = jnp.minimum(pair_sum + 1, 2 * total_rows - 1 - pair_sum)
    distance = jnp.concatenate([near_dist, far_dist], axis=1).astype(jnp.float32)
    weight = jnp.exp(scores * (1.0 / math.sqrt(HS)) - slopes[None, :, None, None] * distance)
    prob = (weight / jnp.sum(weight, axis=-1, keepdims=True)).astype(jnp.bfloat16)
    mixed = jnp.einsum("chrs,schd->rchd", prob, valued, preferred_element_type=jnp.float32)
    return mixed.astype(jnp.bfloat16).reshape(query.shape[0], query.shape[1], -1)


def general(
    fields,
    land_mask,
    land_embed,
    column_gain,
    row_gain,
    column_slopes,
    row_slopes,
    column_project,
    column_output,
    row_project,
    row_output,
):
    lon_count = lax.axis_size("lon")
    lat_count = lax.axis_size("lat")
    band_rows, local_cols, width = fields.shape
    lat_place = lax.axis_index("lat")
    head_total = column_slopes.shape[0]
    head_share = head_total // lat_count
    first_head = lat_place * head_share
    start = fields.astype(jnp.float32) + land_mask.astype(jnp.float32)[..., None] * land_embed
    normed = layer_norm(start, column_gain).astype(jnp.bfloat16)
    whole = gather_bands(normed)
    projected = project_in(whole.reshape(-1, width), column_project)
    query, keyed, valued = head_split(
        projected.reshape(band_rows * lat_count, local_cols, head_share, 3, HS)
    )
    column_kv = jnp.concatenate([keyed, valued], axis=-1).reshape(
        band_rows * lat_count, local_cols, -1
    )
    slopes = lax.dynamic_slice_in_dim(column_slopes, first_head, head_share)
    far_kv = passed_along(column_kv, "lon", lon_count // 2)
    shaped = column_kv.shape[:2] + (head_share, 2 * HS)
    mixed = column_attend(query, column_kv.reshape(shaped), far_kv.reshape(shaped), slopes)
    partial_value = project_out(mixed.reshape(-1, head_share * HS), column_output)
    update = sum_heads(partial_value.reshape(band_rows * lat_count, local_cols, width))
    middle = start + update
    total_rows = band_rows * lat_count
    row_normed = layer_norm(middle, row_gain).astype(jnp.bfloat16)
    whole_rows = gather_bands(row_normed)
    projected = project_in(whole_rows.reshape(-1, width), row_project)
    query, keyed, valued = head_split(projected.reshape(total_rows, local_cols, head_share, 3, HS))
    packed = jnp.stack([query, keyed, valued], axis=3)
    parts = lax.all_to_all(packed, "lon", split_axis=0, concat_axis=1, tiled=True)
    few_rows, all_cols = (parts.shape[0], parts.shape[1])
    scores = jnp.einsum(
        "rchd,rehd->rhce", parts[..., 0, :], parts[..., 1, :], preferred_element_type=jnp.float32
    )
    cols_here = jnp.arange(all_cols, dtype=jnp.int32)
    gap = jnp.abs(cols_here[:, None] - cols_here[None, :])
    cycle_dist = jnp.minimum(gap, all_cols - gap).astype(jnp.float32)
    row_slope = lax.dynamic_slice_in_dim(row_slopes, first_head, head_share)
    weight = jnp.exp(scores * (1.0 / math.sqrt(HS)) - row_slope[None, :, None, None] * cycle_dist)
    prob = (weight / jnp.sum(weight, axis=-1, keepdims=True)).astype(jnp.bfloat16)
    row_mixed = jnp.einsum(
        "rhce,rehd->rchd", prob, parts[..., 2, :], preferred_element_type=jnp.float32
    )
    row_mixed = row_mixed.astype(jnp.bfloat16)
    back = lax.all_to_all(row_mixed, "lon", split_axis=1, concat_axis=0, tiled=True)
    partial_value = project_out(back.reshape(-1, head_share * HS), row_output)
    final_update = sum_heads(partial_value.reshape(total_rows, local_cols, width))
    return (middle + final_update).astype(jnp.bfloat16)


def solution(mesh):
    in_specs = (
        P("lat", "lon", None),
        P("lat", "lon"),
        P(),
        P(),
        P(),
        P(),
        P(),
        P("lon", "lat"),
        P("lon", "lat"),
        P("lon", "lat"),
        P("lon", "lat"),
    )
    out_specs = P(("ens", "lat"), "lon", None)

    def shards(fields, *rest):
        length = lax.axis_size("lon")
        suits = fields.shape[0] % length == 0 and length in (2 * PLANE, 4 * PLANE)
        return (fast if suits else general)(fields, *rest)

    return jax.shard_map(shards, mesh=mesh, in_specs=in_specs, out_specs=out_specs, check_vma=False)
```

```python
import functools
import math

import jax
import jax.numpy as jnp
from jax import lax
from jax.experimental import pallas as pl
from jax.experimental.pallas import tpu as pltpu
from jax.sharding import PartitionSpec as P

HS = 64
PAIR = 2 * HS
PLANE = 4
NEVER = -1e30
EXTRA = 16


def at(place, length):
    return [(i, place(i)) for i in range(length)]


def swap_bands(value):
    return lax.ppermute(value, "lat", at(lambda i: 1 - i, 2))


SCALARS = pl.BlockSpec(memory_space=pltpu.SMEM)


def call(kernel, out, name, scalars, arrays, given=(), scratch=(), room=24, space=pltpu.VMEM):
    return pl.pallas_call(
        kernel,
        out_shape=out,
        in_specs=[SCALARS] * len(scalars)
        + [pl.BlockSpec(memory_space=pltpu.VMEM)] * len(arrays)
        + [pl.BlockSpec(memory_space=pltpu.HBM)] * len(given),
        out_specs=jax.tree.map(lambda _: pl.BlockSpec(memory_space=space), out),
        scratch_shapes=scratch,
        compiler_params=pltpu.CompilerParams(vmem_limit_bytes=room * 2**20),
        cost_estimate=pl.CostEstimate(flops=2**10, bytes_accessed=2**10, transcendentals=0),
        name=name,
    )(*scalars, *arrays, *given)


def dot(a, b):
    return jnp.dot(a, b, preferred_element_type=jnp.float32)


def dot_t(a, b):
    return lax.dot_general(a, b, (((1,), (1,)), ((), ())), preferred_element_type=jnp.float32)


def iota(shape, axis):
    return lax.broadcasted_iota(jnp.int32, shape, axis)


def bring(pairs, sems):
    copies = [pltpu.make_async_copy(ref, held, sems.at[i]) for i, (ref, held) in enumerate(pairs)]
    for copy in copies:
        copy.start()
    return copies


def wait(copies):
    for copy in copies:
        copy.wait()


def along_lines(weight, length):
    steps = range(PLANE, length, PLANE)
    return jnp.concatenate(
        [weight] + [lax.ppermute(weight, "lon", at(lambda i: i ^ k, length)) for k in steps], axis=0
    )


def doubled(weight, step, length):
    got = lax.ppermute(weight, "lon", at(lambda i: i ^ step, length))
    return jnp.concatenate([weight, got], axis=0)


def across_plane(part, length):
    return [part] + [lax.ppermute(part, "lon", at(lambda i: i ^ k, length)) for k in range(1, PLANE)]


def pack_rows_kernel(project, output, out):
    split = project.shape[1]
    out[:, :split] = by_kind(project[...])
    out[:, split:] = output[...]


def by_kind(weight):
    heads = weight.shape[1] // (3 * HS)
    block = lambda kind, head: weight[:, (3 * head + kind) * HS : (3 * head + kind + 1) * HS]
    return jnp.concatenate([block(kind, head) for kind in range(3) for head in range(heads)], axis=1)


def places(shard, place, pieces):
    line, spot = place[0] // PLANE, place[0] % PLANE
    for j, piece in enumerate(pieces):
        for k in range(piece.shape[0] // shard):
            owner = lax.bitwise_xor(line, k) * PLANE + lax.bitwise_xor(spot, j)
            there = pl.ds(pl.multiple_of(owner * shard, shard), shard)
            yield piece, slice(k * shard, (k + 1) * shard), there


def order_kernel(shard, sort, place, w0, w1, w2, w3, out):
    for piece, here, there in places(shard, place, (w0, w1, w2, w3)):
        out[there, :] = by_kind(piece[here, :]) if sort else piece[here, :]


def bring_in_order(shard, place, pieces, lane, target, sems):
    lanes = slice(lane, lane + target.shape[1])
    return bring(
        [
            (piece.at[here, lanes], target.at[there, :])
            for piece, here, there in places(shard, place, pieces)
        ],
        sems,
    )


def norm(values, gain):
    center = values - jnp.mean(values, axis=-1, keepdims=True)
    spread = jnp.mean(center * center, axis=-1, keepdims=True)
    return center * lax.rsqrt(spread + 1e-05) * gain


def land_start(tokens, mask, embed):
    cols, rows = mask.shape
    total = rows * cols
    row_of = (iota((total, rows), 0) // cols == iota((total, rows), 1)).astype(jnp.bfloat16)
    spread = dot_t(row_of, mask.astype(jnp.bfloat16))
    own = iota((total, cols), 0) % cols == iota((total, cols), 1)
    land = jnp.sum(jnp.where(own, spread, 0.0), axis=1, keepdims=True)
    return tokens.astype(jnp.float32).reshape(total, tokens.shape[2]) + land * embed


def packed_start(packed, embed):
    total = packed.shape[0] - EXTRA
    row = packed[total : total + 1, :total].astype(jnp.float32)
    same = iota((total, total), 0) == iota((total, total), 1)
    land = jnp.sum(jnp.where(same, row, 0.0), axis=1, keepdims=True)
    return packed[:total, :].astype(jnp.float32) + land * embed


def slots(cols, rows, side, inverse=False):
    total = cols * rows
    spot, grid = iota((total, total), int(inverse)), iota((total, total), int(not inverse))
    column = lax.rem(spot // rows + side * (cols // 2), cols)
    return (grid == lax.rem(spot, rows) * cols + column).astype(jnp.bfloat16)


def pack_tokens_kernel(lons, place, tokens, mask, keep, send, *scratch):
    *held, sems = scratch
    wait(bring(zip((tokens, mask), held), sems))
    tokens, mask = held
    rows, cols, width = tokens.shape
    half = rows * cols // 2
    side = place[0] // (lons // 2)
    flat = tokens[...].astype(jnp.float32).reshape(rows * cols, width).astype(jnp.bfloat16)
    in_slots = dot(slots(cols, rows, side), flat).astype(jnp.bfloat16)
    land = mask[...].astype(jnp.float32)
    parts = [land[c : c + 1, :] for c in range(cols)]
    halves = [jnp.concatenate(parts[: cols // 2], axis=1), jnp.concatenate(parts[cols // 2 :], axis=1)]
    for k, out in enumerate((keep, send)):
        out[:half, :] = in_slots[k * half : (k + 1) * half]
        out[half:, :] = jnp.zeros((EXTRA, width), jnp.bfloat16)
        row = jnp.where(side == k, halves[0], halves[1])
        out[half:, :half] = jnp.broadcast_to(row, (EXTRA, half)).astype(jnp.bfloat16)


def column_norm_kernel(own, other, far_own, far_other, embed, gain, out):
    half = own.shape[0] - EXTRA
    for k, ref in enumerate((own, other, far_own, far_other)):
        normed = norm(packed_start(ref[...], embed[...]), gain[...])
        out[k * half : (k + 1) * half, :] = normed.astype(jnp.bfloat16)


def unit_heads(vectors, scale=1.0):
    width = vectors.shape[1]
    same = (iota((width, width), 0) // HS == iota((width, width), 1) // HS).astype(jnp.bfloat16)
    total = dot((vectors * vectors).astype(jnp.bfloat16), same)
    return (vectors * (lax.rsqrt(total * (1.0 / HS) + 1e-06) * scale)).astype(jnp.bfloat16)


def two_heads(query, keyed, valued, bias):
    rows = query.shape[0]
    first = iota(query.shape, 1) < HS
    zero = jnp.zeros_like(query)
    stacked = jnp.concatenate([jnp.where(first, query, zero), jnp.where(first, zero, query)], axis=0)
    weight = jnp.exp(dot_t(stacked, keyed) + bias).astype(jnp.bfloat16)
    widened = jnp.concatenate([valued, jnp.ones_like(valued)], axis=1)
    mixed = dot(weight, widened)
    mixed = mixed[:, :PAIR] / mixed[:, PAIR:]
    return jnp.where(first, mixed[:rows], mixed[rows:]).astype(jnp.bfloat16)


def column_kernel(band, place, slopes, tokens, weight, out_own, out_other, qkv):
    block = tokens.shape[0] // 4
    loops = block // band
    width = weight.shape[1] // 3
    projected = dot(tokens[...], weight[...])
    qkv[:, :width] = unit_heads(projected[:, :width], 1.0 / math.sqrt(HS))
    qkv[:, width : 2 * width] = unit_heads(projected[:, width : 2 * width])
    qkv[:, 2 * width :] = projected[:, 2 * width :].astype(jnp.bfloat16)
    total = 2 * band
    shape = (2 * total, 2 * total)
    spot_q, spot_k = iota(shape, 0), iota(shape, 1)
    shift = place[1] * band
    row_q, row_k = lax.rem(spot_q + shift, total), lax.rem(spot_k + shift, total)
    pair_sum = row_q + row_k
    beyond = jnp.minimum(pair_sum + 1, 2 * total - 1 - pair_sum)
    here = (spot_q < total) == (spot_k < total)
    distance = jnp.where(here, jnp.abs(row_q - row_k), beyond).astype(jnp.float32)
    first = place[1] * (width // HS)
    for pair in range(width // PAIR):
        bias = jnp.concatenate(
            [distance * -slopes[first + 2 * pair + one] for one in range(2)], axis=0
        )
        lanes = slice(pair * PAIR, (pair + 1) * PAIR)
        for loop in range(loops):
            starts = [part * block + loop * band for part in range(4)]
            query, keyed, valued = (
                jnp.concatenate(
                    [
                        qkv[at : at + band, kind * width + lanes.start : kind * width + lanes.stop]
                        for at in starts
                    ],
                    axis=0,
                )
                for kind in range(3)
            )
            mixed = two_heads(query, keyed, valued, bias)
            for part in range(4):
                out = (out_own, out_other)[part % 2]
                slot = (part // 2) * loops + loop
                out[slot * band : (slot + 1) * band, lanes] = mixed[part * band : (part + 1) * band]


def middle_kernel(cols, mine, theirs, near, far, kept, got, embed, gain, out):
    update = dot_t(mine[...], near[...]) + dot_t(theirs[...], far[...])
    parts = [packed_start(ref[...], embed[...]) for ref in (kept, got)]
    middle = jnp.concatenate(parts, axis=0) + update
    normed = norm(middle, gain[...]).astype(jnp.bfloat16)
    by_row = slots(cols, normed.shape[0] // cols, 0, True)
    out[...] = dot(by_row, normed).astype(jnp.bfloat16)


def home_kernel(lons, place, mine, theirs, back, near, far, tokens, mask, embed, out, *scratch):
    *held, total, sems = scratch
    coming = bring(zip((tokens, mask, embed), held), sems)
    tokens, mask, embed = held
    rows, cols, _ = tokens.shape
    half, width = rows * cols // 2, near.shape[1]
    to_grid = slots(cols, rows, place[0] // (lons // 2), True)
    update = 0.0
    for lane, (kept, weight) in enumerate(((mine, near), (theirs, far))):
        mixed = dot(to_grid[:, :half], kept[:half, :])
        mixed += dot(to_grid[:, half:], back[:, lane * width : (lane + 1) * width])
        update += dot_t(mixed.astype(jnp.bfloat16), weight[...])
    wait(coming)
    total[...] = land_start(tokens[...], mask[...], embed[...]) + update
    wait(bring([(total, out)], sems))


def row_kernel(shard, cols, rows, place, slopes, tokens, *refs):
    pieces, (out, weight, sems) = refs[:-3], refs[-3:]
    coming = [
        bring_in_order(
            shard, place, pieces[half * PLANE : (half + 1) * PLANE], 0, weight.at[half], sems.at[half]
        )
        for half in range(2)
    ]
    total = tokens.shape[0]
    block = cols * rows
    lon_count = total // block
    circle = lon_count * cols
    turn, part = lon_count // 2, cols // 2
    spot_q, spot_k = iota((total, total), 0), iota((total, total), 1)

    def lon_of(spot):
        device, slot = spot // block, lax.rem(spot, cols)
        side = device // turn
        holder = lax.rem(device + (slot // part) * turn, lon_count)
        return holder * cols + side * part + lax.rem(slot, part)

    row_of = lambda spot: lax.rem(spot, block) // cols
    gap = jnp.abs(lon_of(spot_q) - lon_of(spot_k))
    distance = jnp.minimum(gap, circle - gap).astype(jnp.float32)
    column = lax.rem(spot_q, cols)
    away = (column // part != spot_q // block // turn).astype(jnp.int32)
    home = lax.rem(spot_q // block + away * turn, lon_count) * block
    home = home + row_of(spot_q) * cols + away * part + lax.rem(column, part)
    homeward = (spot_k == home).astype(jnp.bfloat16)
    same = row_of(spot_q) == row_of(spot_k)
    width = weight.shape[2] // 3
    heads = width // HS
    for half in range(2):
        first = lax.rem(place[1] + half, 2) * heads
        wait(coming[half])
        projected = dot(tokens[...], weight[half])
        query = unit_heads(projected[:, :width], 1.0 / math.sqrt(HS))
        keyed = unit_heads(projected[:, width : 2 * width])
        valued = projected[:, 2 * width :].astype(jnp.bfloat16)
        for pair in range(width // PAIR):
            lanes = slice(pair * PAIR, (pair + 1) * PAIR)
            bias = jnp.concatenate(
                [
                    jnp.where(same, distance * -slopes[first + 2 * pair + one], NEVER)
                    for one in range(2)
                ],
                axis=0,
            )
            mixed = two_heads(query[:, lanes], keyed[:, lanes], valued[:, lanes], bias)
            start = half * width + pair * PAIR
            out[:, start : start + PAIR] = dot(homeward, mixed).astype(jnp.bfloat16)


def final_kernel(shard, place, mixed, *refs):
    pieces, middle, out, weight, total, sems, total_sems = refs[:-6], *refs[-6:]
    width = weight.shape[2]
    lane = pieces[0].shape[1] - width
    coming = [
        bring_in_order(
            shard, place, pieces[half * PLANE : (half + 1) * PLANE], lane, weight.at[half], sems.at[half]
        )
        for half in range(2)
    ]
    rows = total.shape[0] // 4
    cut = [slice(i * rows, (i + 1) * rows) for i in range(4)]
    last = bring([(middle.at[here, :], total.at[here, :]) for here in cut], total_sems)
    update = 0.0
    for half in range(2):
        wait(coming[half])
        update += dot_t(mixed[:, half * width : (half + 1) * width], weight[half])
    wait(last)
    out[...] = (total[...] + update).reshape(out.shape).astype(jnp.bfloat16)


def fast(
    fields,
    land_mask,
    land_embed,
    column_gain,
    row_gain,
    column_slopes,
    row_slopes,
    column_project,
    column_output,
    row_project,
    row_output,
):
    lon_count = lax.axis_size("lon")
    lat = lax.axis_index("lat")
    lon = lax.axis_index("lon")
    band, cols, width = fields.shape
    tokens = band * cols
    heads = column_slopes.shape[0]
    half = heads // 2
    attend = half * HS
    shard = column_project.shape[0]
    place = jnp.stack([lon, lat]).astype(jnp.int32)
    embed, column_gain, row_gain = (v.reshape(1, width) for v in (land_embed, column_gain, row_gain))
    bf16 = lambda *shape: jax.ShapeDtypeStruct(shape, jnp.bfloat16)
    f32 = lambda *shape: jax.ShapeDtypeStruct(shape, jnp.float32)
    rows = shard * lon_count
    weights = (bf16(rows, 3 * attend), bf16(rows, attend))

    order = lambda pieces, name, sort, out: call(
        functools.partial(order_kernel, shard, sort), out, name, (place,), pieces
    )
    project_shape, output_shape = weights
    antipode = lambda value: lax.ppermute(
        value, "lon", at(lambda i: (i + lon_count // 2) % lon_count, lon_count)
    )
    packed = bf16(tokens // 2 + EXTRA, width)
    mask = land_mask.T
    held = [pltpu.VMEM(fields.shape, fields.dtype), pltpu.VMEM(mask.shape, mask.dtype)]

    first = along_lines(column_project, lon_count)
    keep, send = call(
        functools.partial(pack_tokens_kernel, lon_count),
        (packed, packed),
        "loop_tokens",
        (place,),
        (),
        (fields, mask),
        held + [pltpu.SemaphoreType.DMA((2,))],
        room=60,
    )
    second = column_output
    third = bf16(shard, row_project.shape[1] + row_output.shape[1])
    third = call(pack_rows_kernel, third, "row_shards", (), (row_project, row_output))
    if lon_count > PLANE:
        second = doubled(second, PLANE, lon_count)
        third = doubled(third, PLANE, lon_count)
    keep_other = swap_bands(keep)
    first, second, third, send = lax.optimization_barrier((first, second, third, send))
    far = antipode(send)
    pieces = across_plane(first, lon_count)
    if lon_count > 2 * PLANE:
        second = doubled(second, 2 * PLANE, lon_count)
    far_other = swap_bands(far)
    normed = call(
        column_norm_kernel,
        bf16(2 * tokens, width),
        "column_normed",
        (),
        (keep, keep_other, far, far_other, embed, column_gain),
    )
    normed, pieces, second = lax.optimization_barrier((normed, pieces, second))
    third, _ = lax.optimization_barrier((third, far))
    project = order(pieces, "column_project", True, project_shape)
    second = across_plane(second, lon_count)
    if lon_count > 2 * PLANE:
        third = doubled(third, 2 * PLANE, lon_count)

    mixed_own, mixed_other = call(
        functools.partial(column_kernel, band),
        (bf16(tokens, attend), bf16(tokens, attend)),
        "column_attention",
        (place, column_slopes),
        (normed, project),
        (),
        [pltpu.VMEM((2 * tokens, 3 * attend), jnp.bfloat16)],
    )
    theirs = swap_bands(mixed_other)
    second, third, mixed_own = lax.optimization_barrier((second, third, mixed_own))
    output = order(second, "column_output", False, output_shape)
    output_far = swap_bands(output)
    third = across_plane(third, lon_count)
    back = antipode(jnp.concatenate([mixed_own[tokens // 2 :], theirs[tokens // 2 :]], axis=1))
    row_normed = call(
        functools.partial(middle_kernel, cols),
        bf16(tokens, width),
        "row_normed",
        (),
        (mixed_own, theirs, output, output_far, keep, far, embed, row_gain),
    )
    spread = lax.all_to_all(row_normed, "lon", split_axis=0, concat_axis=0, tiled=True)
    third, back = lax.optimization_barrier((third, back))
    third_far = [swap_bands(piece) for piece in third]
    middle = call(
        functools.partial(home_kernel, lon_count),
        f32(tokens, width),
        "middle",
        (place,),
        (mixed_own, theirs, back, output, output_far),
        (fields, mask, embed),
        held + [pltpu.VMEM(embed.shape, embed.dtype), pltpu.VMEM((tokens, width), jnp.float32)]
        + [pltpu.SemaphoreType.DMA((3,))],
        space=pltpu.HBM,
    )
    sems = pltpu.SemaphoreType.DMA((2, lon_count))
    row_mixed = call(
        functools.partial(row_kernel, shard, cols, band // lon_count),
        bf16(tokens, 2 * attend),
        "row_attention",
        (place, row_slopes),
        (spread,),
        (*third, *third_far),
        [pltpu.VMEM((2, *project_shape.shape), jnp.bfloat16), sems],
        room=60,
    )
    back = lax.all_to_all(row_mixed, "lon", split_axis=0, concat_axis=0, tiled=True)
    return call(
        functools.partial(final_kernel, shard),
        bf16(band, cols, width),
        "block_output",
        (place,),
        (back,),
        (*third, *third_far, middle),
        [
            pltpu.VMEM((2, *output_shape.shape), jnp.bfloat16),
            pltpu.VMEM((tokens, width), jnp.float32),
            sems,
            pltpu.SemaphoreType.DMA((4,)),
        ],
        room=60,
    )


def passed_along(value, axis, by):
    length = lax.axis_size(axis)
    return lax.ppermute(value, axis, [(i, (i + by) % length) for i in range(length)])


def layer_norm(values, gain):
    center = values - jnp.mean(values, axis=-1, keepdims=True)
    spread = jnp.mean(center * center, axis=-1, keepdims=True)
    return center * lax.rsqrt(spread + 1e-05) * gain


def unit_rms(vectors):
    return vectors * lax.rsqrt(jnp.mean(vectors * vectors, axis=-1, keepdims=True) + 1e-06)


def head_split(projected):
    query = unit_rms(projected[..., 0, :]).astype(jnp.bfloat16)
    keyed = unit_rms(projected[..., 1, :]).astype(jnp.bfloat16)
    valued = projected[..., 2, :].astype(jnp.bfloat16)
    return (query, keyed, valued)


def gather_bands(normed):
    return lax.all_gather(normed, "lat", axis=0, tiled=True)


def sum_heads(partial_value):
    return lax.psum_scatter(
        partial_value.astype(jnp.bfloat16), "lat", scatter_dimension=0, tiled=True
    ).astype(jnp.float32)


def project_in(normed, weight):
    return jnp.dot(
        normed,
        lax.all_gather(weight, "lon", axis=0, tiled=True),
        preferred_element_type=jnp.float32,
    )


def project_out(mixed, weight):
    return lax.dot_general(
        mixed,
        lax.all_gather(weight, "lon", axis=0, tiled=True),
        (((1,), (1,)), ((), ())),
        preferred_element_type=jnp.float32,
    )


def column_attend(query, column_kv, far_kv, slopes):
    total_rows = column_kv.shape[0]
    keyed = jnp.concatenate([column_kv[..., :HS], far_kv[..., :HS]], axis=0)
    valued = jnp.concatenate([column_kv[..., HS:], far_kv[..., HS:]], axis=0)
    scores = jnp.einsum("rchd,schd->chrs", query, keyed, preferred_element_type=jnp.float32)
    rows_here = jnp.arange(query.shape[0], dtype=jnp.int32)
    key_rows = jnp.arange(total_rows, dtype=jnp.int32)
    near_dist = jnp.abs(rows_here[:, None] - key_rows[None, :])
    pair_sum = rows_here[:, None] + key_rows[None, :]
    far_dist = jnp.minimum(pair_sum + 1, 2 * total_rows - 1 - pair_sum)
    distance = jnp.concatenate([near_dist, far_dist], axis=1).astype(jnp.float32)
    weight = jnp.exp(scores * (1.0 / math.sqrt(HS)) - slopes[None, :, None, None] * distance)
    prob = (weight / jnp.sum(weight, axis=-1, keepdims=True)).astype(jnp.bfloat16)
    mixed = jnp.einsum("chrs,schd->rchd", prob, valued, preferred_element_type=jnp.float32)
    return mixed.astype(jnp.bfloat16).reshape(query.shape[0], query.shape[1], -1)


def general(
    fields,
    land_mask,
    land_embed,
    column_gain,
    row_gain,
    column_slopes,
    row_slopes,
    column_project,
    column_output,
    row_project,
    row_output,
):
    lon_count = lax.axis_size("lon")
    lat_count = lax.axis_size("lat")
    band_rows, local_cols, width = fields.shape
    lat_place = lax.axis_index("lat")
    head_total = column_slopes.shape[0]
    head_share = head_total // lat_count
    first_head = lat_place * head_share
    start = fields.astype(jnp.float32) + land_mask.astype(jnp.float32)[..., None] * land_embed
    normed = layer_norm(start, column_gain).astype(jnp.bfloat16)
    whole = gather_bands(normed)
    projected = project_in(whole.reshape(-1, width), column_project)
    query, keyed, valued = head_split(
        projected.reshape(band_rows * lat_count, local_cols, head_share, 3, HS)
    )
    column_kv = jnp.concatenate([keyed, valued], axis=-1).reshape(
        band_rows * lat_count, local_cols, -1
    )
    slopes = lax.dynamic_slice_in_dim(column_slopes, first_head, head_share)
    far_kv = passed_along(column_kv, "lon", lon_count // 2)
    shaped = column_kv.shape[:2] + (head_share, 2 * HS)
    mixed = column_attend(query, column_kv.reshape(shaped), far_kv.reshape(shaped), slopes)
    partial_value = project_out(mixed.reshape(-1, head_share * HS), column_output)
    update = sum_heads(partial_value.reshape(band_rows * lat_count, local_cols, width))
    middle = start + update
    total_rows = band_rows * lat_count
    row_normed = layer_norm(middle, row_gain).astype(jnp.bfloat16)
    whole_rows = gather_bands(row_normed)
    projected = project_in(whole_rows.reshape(-1, width), row_project)
    query, keyed, valued = head_split(projected.reshape(total_rows, local_cols, head_share, 3, HS))
    packed = jnp.stack([query, keyed, valued], axis=3)
    parts = lax.all_to_all(packed, "lon", split_axis=0, concat_axis=1, tiled=True)
    few_rows, all_cols = (parts.shape[0], parts.shape[1])
    scores = jnp.einsum(
        "rchd,rehd->rhce", parts[..., 0, :], parts[..., 1, :], preferred_element_type=jnp.float32
    )
    cols_here = jnp.arange(all_cols, dtype=jnp.int32)
    gap = jnp.abs(cols_here[:, None] - cols_here[None, :])
    cycle_dist = jnp.minimum(gap, all_cols - gap).astype(jnp.float32)
    row_slope = lax.dynamic_slice_in_dim(row_slopes, first_head, head_share)
    weight = jnp.exp(scores * (1.0 / math.sqrt(HS)) - row_slope[None, :, None, None] * cycle_dist)
    prob = (weight / jnp.sum(weight, axis=-1, keepdims=True)).astype(jnp.bfloat16)
    row_mixed = jnp.einsum(
        "rhce,rehd->rchd", prob, parts[..., 2, :], preferred_element_type=jnp.float32
    )
    row_mixed = row_mixed.astype(jnp.bfloat16)
    back = lax.all_to_all(row_mixed, "lon", split_axis=1, concat_axis=0, tiled=True)
    partial_value = project_out(back.reshape(-1, head_share * HS), row_output)
    final_update = sum_heads(partial_value.reshape(total_rows, local_cols, width))
    return (middle + final_update).astype(jnp.bfloat16)


def solution(mesh):
    in_specs = (
        P("lat", "lon", None),
        P("lat", "lon"),
        P(),
        P(),
        P(),
        P(),
        P(),
        P("lon", "lat"),
        P("lon", "lat"),
        P("lon", "lat"),
        P("lon", "lat"),
    )
    out_specs = P(("ens", "lat"), "lon", None)

    def shards(fields, *rest):
        length = lax.axis_size("lon")
        suits = fields.shape[0] % length == 0 and length in (2 * PLANE, 4 * PLANE)
        return (fast if suits else general)(fields, *rest)

    return jax.shard_map(shards, mesh=mesh, in_specs=in_specs, out_specs=out_specs, check_vma=False)
```

```python
import functools
import math

import jax
import jax.numpy as jnp
from jax import lax
from jax.experimental import pallas as pl
from jax.experimental.pallas import tpu as pltpu
from jax.sharding import PartitionSpec as P

HS = 64
PAIR = 2 * HS
PLANE = 4
NEVER = -1e30
EXTRA = 16


def at(place, length):
    return [(i, place(i)) for i in range(length)]


def swap_bands(value):
    return lax.ppermute(value, "lat", at(lambda i: 1 - i, 2))


SCALARS = pl.BlockSpec(memory_space=pltpu.SMEM)


def call(kernel, out, name, scalars, arrays, given=(), scratch=(), cost=2**10, room=24, space=pltpu.VMEM):
    return pl.pallas_call(
        kernel,
        out_shape=out,
        in_specs=[SCALARS] * len(scalars)
        + [pl.BlockSpec(memory_space=pltpu.VMEM)] * len(arrays)
        + [pl.BlockSpec(memory_space=pltpu.HBM)] * len(given),
        out_specs=jax.tree.map(lambda _: pl.BlockSpec(memory_space=space), out),
        scratch_shapes=scratch,
        compiler_params=pltpu.CompilerParams(vmem_limit_bytes=room * 2**20),
        cost_estimate=pl.CostEstimate(flops=2**10, bytes_accessed=cost, transcendentals=0),
        name=name,
    )(*scalars, *arrays, *given)


def dot(a, b):
    return jnp.dot(a, b, preferred_element_type=jnp.float32)


def dot_t(a, b):
    return lax.dot_general(a, b, (((1,), (1,)), ((), ())), preferred_element_type=jnp.float32)


def iota(shape, axis):
    return lax.broadcasted_iota(jnp.int32, shape, axis)


def bring(pairs, sems):
    copies = [pltpu.make_async_copy(ref, held, sems.at[i]) for i, (ref, held) in enumerate(pairs)]
    for copy in copies:
        copy.start()
    return copies


def wait(copies):
    for copy in copies:
        copy.wait()


def along_lines(weight, length):
    steps = range(PLANE, length, PLANE)
    return jnp.concatenate(
        [weight] + [lax.ppermute(weight, "lon", at(lambda i: i ^ k, length)) for k in steps], axis=0
    )


def doubled(weight, step, length):
    got = lax.ppermute(weight, "lon", at(lambda i: i ^ step, length))
    return jnp.concatenate([weight, got], axis=0)


def across_plane(part, length):
    return [part] + [lax.ppermute(part, "lon", at(lambda i: i ^ k, length)) for k in range(1, PLANE)]


def relayed_plane(part, length):
    half = part.shape[0] // 2
    step = lambda value, k: lax.ppermute(value, "lon", at(lambda i: i ^ k, length))
    first, second = step(part, 1), step(part, 2)
    return [part, first, second], [step(second[:half], 1), step(first[half:], 2)]


def by_kind(weight):
    heads = weight.shape[1] // (3 * HS)
    block = lambda kind, head: weight[:, (3 * head + kind) * HS : (3 * head + kind + 1) * HS]
    return jnp.concatenate([block(kind, head) for kind in range(3) for head in range(heads)], axis=1)


def places(shard, place, pieces):
    line, spot = place[0] // PLANE, place[0] % PLANE
    lines = pieces[0].shape[0] // shard
    blocks = [(piece, k) for piece in pieces for k in range(piece.shape[0] // shard)]
    for number, (piece, k) in enumerate(blocks):
        owner = lax.bitwise_xor(line, number % lines) * PLANE
        owner += lax.bitwise_xor(spot, number // lines)
        there = pl.ds(pl.multiple_of(owner * shard, shard), shard)
        yield piece, slice(k * shard, (k + 1) * shard), there


def order_kernel(shard, sort, place, w0, w1, w2, w3, out):
    for piece, here, there in places(shard, place, (w0, w1, w2, w3)):
        out[there, :] = by_kind(piece[here, :]) if sort else piece[here, :]


def bring_in_order(shard, place, pieces, lane, target, sems):
    lanes = slice(lane, lane + target.shape[1])
    return bring(
        [
            (piece.at[here, lanes], target.at[there, :])
            for piece, here, there in places(shard, place, pieces)
        ],
        sems,
    )


def norm(values, gain):
    center = values - jnp.mean(values, axis=-1, keepdims=True)
    spread = jnp.mean(center * center, axis=-1, keepdims=True)
    return center * lax.rsqrt(spread + 1e-05) * gain


def land_start(tokens, mask, embed):
    cols, rows = mask.shape
    total = rows * cols
    row_of = (iota((total, rows), 0) // cols == iota((total, rows), 1)).astype(jnp.bfloat16)
    spread = dot_t(row_of, mask.astype(jnp.bfloat16))
    own = iota((total, cols), 0) % cols == iota((total, cols), 1)
    land = jnp.sum(jnp.where(own, spread, 0.0), axis=1, keepdims=True)
    return tokens.astype(jnp.float32).reshape(total, tokens.shape[2]) + land * embed


def packed_start(packed, embed):
    total = packed.shape[0] - EXTRA
    row = packed[total : total + 1, :total].astype(jnp.float32)
    same = iota((total, total), 0) == iota((total, total), 1)
    land = jnp.sum(jnp.where(same, row, 0.0), axis=1, keepdims=True)
    return packed[:total, :].astype(jnp.float32) + land * embed


def slots(cols, rows, side, inverse=False):
    total = cols * rows
    spot, grid = iota((total, total), int(inverse)), iota((total, total), int(not inverse))
    column = lax.rem(spot // rows + side * (cols // 2), cols)
    return (grid == lax.rem(spot, rows) * cols + column).astype(jnp.bfloat16)


def first_kernel(lons, place, tokens, mask, project, output, keep, send, packed, *scratch):
    *held, sems = scratch
    coming = bring(zip((tokens, mask, project, output), held), sems)
    tokens, mask, project, output = held
    rows, cols, width = tokens.shape
    half = rows * cols // 2
    side = place[0] // (lons // 2)
    to_slots = slots(cols, rows, side)
    wait(coming[:2])
    flat = tokens[...].astype(jnp.float32).reshape(rows * cols, width).astype(jnp.bfloat16)
    in_slots = dot(to_slots, flat).astype(jnp.bfloat16)
    land = mask[...].astype(jnp.float32)
    parts = [land[c : c + 1, :] for c in range(cols)]
    halves = [jnp.concatenate(parts[: cols // 2], axis=1), jnp.concatenate(parts[cols // 2 :], axis=1)]
    for k, out in enumerate((keep, send)):
        out[:half, :] = in_slots[k * half : (k + 1) * half]
        out[half:, :] = jnp.zeros((EXTRA, width), jnp.bfloat16)
        row = jnp.where(side == k, halves[0], halves[1])
        out[half:, :half] = jnp.broadcast_to(row, (EXTRA, half)).astype(jnp.bfloat16)
    wait(coming[2:])
    split = project.shape[1]
    packed[:, :split] = by_kind(project[...])
    packed[:, split:] = output[...]


def column_norm_kernel(own, other, far_own, far_other, embed, gain, out):
    half = own.shape[0] - EXTRA
    for k, ref in enumerate((own, other, far_own, far_other)):
        normed = norm(packed_start(ref[...], embed[...]), gain[...])
        out[k * half : (k + 1) * half, :] = normed.astype(jnp.bfloat16)


def unit_heads(vectors, scale=1.0):
    width = vectors.shape[1]
    same = (iota((width, width), 0) // HS == iota((width, width), 1) // HS).astype(jnp.bfloat16)
    total = dot((vectors * vectors).astype(jnp.bfloat16), same)
    return (vectors * (lax.rsqrt(total * (1.0 / HS) + 1e-06) * scale)).astype(jnp.bfloat16)


def two_heads(query, keyed, valued, bias):
    rows = query.shape[0]
    first = iota(query.shape, 1) < HS
    zero = jnp.zeros_like(query)
    stacked = jnp.concatenate([jnp.where(first, query, zero), jnp.where(first, zero, query)], axis=0)
    weight = jnp.exp(dot_t(stacked, keyed) + bias).astype(jnp.bfloat16)
    widened = jnp.concatenate([valued, jnp.ones_like(valued)], axis=1)
    mixed = dot(weight, widened)
    mixed = mixed[:, :PAIR] / mixed[:, PAIR:]
    return jnp.where(first, mixed[:rows], mixed[rows:]).astype(jnp.bfloat16)


def column_kernel(band, place, slopes, tokens, weight, out_own, out_other, qkv):
    block = tokens.shape[0] // 4
    loops = block // band
    width = weight.shape[1] // 3
    projected = dot(tokens[...], weight[...])
    qkv[:, :width] = unit_heads(projected[:, :width], 1.0 / math.sqrt(HS))
    qkv[:, width : 2 * width] = unit_heads(projected[:, width : 2 * width])
    qkv[:, 2 * width :] = projected[:, 2 * width :].astype(jnp.bfloat16)
    total = 2 * band
    shape = (2 * total, 2 * total)
    spot_q, spot_k = iota(shape, 0), iota(shape, 1)
    shift = place[1] * band
    row_q, row_k = lax.rem(spot_q + shift, total), lax.rem(spot_k + shift, total)
    pair_sum = row_q + row_k
    beyond = jnp.minimum(pair_sum + 1, 2 * total - 1 - pair_sum)
    here = (spot_q < total) == (spot_k < total)
    distance = jnp.where(here, jnp.abs(row_q - row_k), beyond).astype(jnp.float32)
    first = place[1] * (width // HS)
    for pair in range(width // PAIR):
        bias = jnp.concatenate(
            [distance * -slopes[first + 2 * pair + one] for one in range(2)], axis=0
        )
        lanes = slice(pair * PAIR, (pair + 1) * PAIR)
        for loop in range(loops):
            starts = [part * block + loop * band for part in range(4)]
            query, keyed, valued = (
                jnp.concatenate(
                    [
                        qkv[at : at + band, kind * width + lanes.start : kind * width + lanes.stop]
                        for at in starts
                    ],
                    axis=0,
                )
                for kind in range(3)
            )
            mixed = two_heads(query, keyed, valued, bias)
            for part in range(4):
                out = (out_own, out_other)[part % 2]
                slot = (part // 2) * loops + loop
                out[slot * band : (slot + 1) * band, lanes] = mixed[part * band : (part + 1) * band]


def middle_kernel(cols, mine, theirs, near, far, kept, got, embed, gain, out):
    update = dot_t(mine[...], near[...]) + dot_t(theirs[...], far[...])
    parts = [packed_start(ref[...], embed[...]) for ref in (kept, got)]
    middle = jnp.concatenate(parts, axis=0) + update
    normed = norm(middle, gain[...]).astype(jnp.bfloat16)
    by_row = slots(cols, normed.shape[0] // cols, 0, True)
    out[...] = dot(by_row, normed).astype(jnp.bfloat16)


def home_kernel(shard, lons, place, mine, theirs, back, near, far, *refs):
    pieces, (tokens, mask, embed, out, out_weight, *held, weight_sems, sems) = refs[:-10], refs[-10:]
    lane = pieces[0].shape[1] - out_weight.shape[2]
    coming = bring(zip((tokens, mask, embed), held), sems)
    count = len(pieces) // 2
    later = []
    for half in range(2):
        mine_of = pieces[half * count : (half + 1) * count]
        later += bring_in_order(shard, place, mine_of, lane, out_weight.at[half], weight_sems.at[half])
    tokens, mask, embed = held
    rows, cols, _ = tokens.shape
    half, width = rows * cols // 2, near.shape[1]
    to_grid = slots(cols, rows, place[0] // (lons // 2), True)
    update = 0.0
    for lane, (kept, weight) in enumerate(((mine, near), (theirs, far))):
        mixed = dot(to_grid[:, :half], kept[:half, :])
        mixed += dot(to_grid[:, half:], back[:, lane * width : (lane + 1) * width])
        update += dot_t(mixed.astype(jnp.bfloat16), weight[...])
    wait(coming)
    out[...] = land_start(tokens[...], mask[...], embed[...]) + update
    wait(later)


def row_kernel(shard, cols, rows, place, slopes, tokens, *refs):
    pieces, (out, weight, sems) = refs[:-3], refs[-3:]
    coming = [
        bring_in_order(
            shard, place, pieces[half * len(pieces) // 2 : (half + 1) * len(pieces) // 2], 0, weight.at[half], sems.at[half]
        )
        for half in range(2)
    ]
    total = tokens.shape[0]
    block = cols * rows
    lon_count = total // block
    circle = lon_count * cols
    turn, part = lon_count // 2, cols // 2
    spot_q, spot_k = iota((total, total), 0), iota((total, total), 1)

    def lon_of(spot):
        device, slot = spot // block, lax.rem(spot, cols)
        side = device // turn
        holder = lax.rem(device + (slot // part) * turn, lon_count)
        return holder * cols + side * part + lax.rem(slot, part)

    row_of = lambda spot: lax.rem(spot, block) // cols
    gap = jnp.abs(lon_of(spot_q) - lon_of(spot_k))
    distance = jnp.minimum(gap, circle - gap).astype(jnp.float32)
    column = lax.rem(spot_q, cols)
    away = (column // part != spot_q // block // turn).astype(jnp.int32)
    home = lax.rem(spot_q // block + away * turn, lon_count) * block
    home = home + row_of(spot_q) * cols + away * part + lax.rem(column, part)
    homeward = (spot_k == home).astype(jnp.bfloat16)
    same = row_of(spot_q) == row_of(spot_k)
    width = weight.shape[2] // 3
    heads = width // HS
    for half in range(2):
        first = lax.rem(place[1] + half, 2) * heads
        wait(coming[half])
        projected = dot(tokens[...], weight[half])
        query = unit_heads(projected[:, :width], 1.0 / math.sqrt(HS))
        keyed = unit_heads(projected[:, width : 2 * width])
        valued = projected[:, 2 * width :].astype(jnp.bfloat16)
        for pair in range(width // PAIR):
            lanes = slice(pair * PAIR, (pair + 1) * PAIR)
            bias = jnp.concatenate(
                [
                    jnp.where(same, distance * -slopes[first + 2 * pair + one], NEVER)
                    for one in range(2)
                ],
                axis=0,
            )
            mixed = two_heads(query[:, lanes], keyed[:, lanes], valued[:, lanes], bias)
            start = half * width + pair * PAIR
            out[:, start : start + PAIR] = dot(homeward, mixed).astype(jnp.bfloat16)


def final_kernel(middle, mixed, weight, out):
    width = weight.shape[2]
    update = dot_t(mixed[:, :width], weight[0]) + dot_t(mixed[:, width:], weight[1])
    out[...] = (middle[...] + update).reshape(out.shape).astype(jnp.bfloat16)


def fast(
    fields,
    land_mask,
    land_embed,
    column_gain,
    row_gain,
    column_slopes,
    row_slopes,
    column_project,
    column_output,
    row_project,
    row_output,
):
    lon_count = lax.axis_size("lon")
    lat = lax.axis_index("lat")
    lon = lax.axis_index("lon")
    band, cols, width = fields.shape
    tokens = band * cols
    heads = column_slopes.shape[0]
    half = heads // 2
    attend = half * HS
    shard = column_project.shape[0]
    place = jnp.stack([lon, lat]).astype(jnp.int32)
    embed, column_gain, row_gain = (v.reshape(1, width) for v in (land_embed, column_gain, row_gain))
    bf16 = lambda *shape: jax.ShapeDtypeStruct(shape, jnp.bfloat16)
    f32 = lambda *shape: jax.ShapeDtypeStruct(shape, jnp.float32)
    rows = shard * lon_count
    weights = (bf16(rows, 3 * attend), bf16(rows, attend))

    order = lambda pieces, name, sort, out: call(
        functools.partial(order_kernel, shard, sort), out, name, (place,), pieces
    )
    project_shape, output_shape = weights
    antipode = lambda value: lax.ppermute(
        value, "lon", at(lambda i: (i + lon_count // 2) % lon_count, lon_count)
    )
    packed = bf16(tokens // 2 + EXTRA, width)
    mask = land_mask.T

    first = along_lines(column_project, lon_count)
    third = bf16(shard, row_project.shape[1] + row_output.shape[1])
    given = (fields, mask, row_project, row_output)
    keep, send, third = call(
        functools.partial(first_kernel, lon_count),
        (packed, packed, third),
        "loop_tokens",
        (place,),
        (),
        given,
        [pltpu.VMEM(v.shape, v.dtype) for v in given] + [pltpu.SemaphoreType.DMA((4,))],
        room=60,
    )
    second = column_output
    if lon_count > PLANE:
        second = doubled(second, PLANE, lon_count)
        third = doubled(third, PLANE, lon_count)
    keep_other = swap_bands(keep)
    far = antipode(send)
    first, second, third, keep_other = lax.optimization_barrier((first, second, third, keep_other))
    pieces = across_plane(first, lon_count)
    if lon_count > 2 * PLANE:
        second = doubled(second, 2 * PLANE, lon_count)
    far_other = swap_bands(far)
    normed = call(
        column_norm_kernel,
        bf16(2 * tokens, width),
        "column_normed",
        (),
        (keep, keep_other, far, far_other, embed, column_gain),
    )
    project = order(pieces, "column_project", True, project_shape)
    normed, project, second = lax.optimization_barrier((normed, project, second))
    third, _ = lax.optimization_barrier((third, far))
    second = across_plane(second, lon_count)
    if lon_count > 2 * PLANE:
        third = doubled(third, 2 * PLANE, lon_count)

    mixed_own, mixed_other = call(
        functools.partial(column_kernel, band),
        (bf16(tokens, attend), bf16(tokens, attend)),
        "column_attention",
        (place, column_slopes),
        (normed, project),
        (),
        [pltpu.VMEM((2 * tokens, 3 * attend), jnp.bfloat16)],
        cost=1 * 2**18,
    )
    theirs = swap_bands(mixed_other)
    second, third, mixed_own = lax.optimization_barrier((second, third, mixed_own))
    output = order(second, "column_output", False, output_shape)
    output_far = swap_bands(output)
    third, late = relayed_plane(third, lon_count)
    to_home = jnp.concatenate([mixed_own[tokens // 2 :], theirs[tokens // 2 :]], axis=1)
    row_normed = call(
        functools.partial(middle_kernel, cols),
        bf16(tokens, width),
        "row_normed",
        (),
        (mixed_own, theirs, output, output_far, keep, far, embed, row_gain),
    )
    spread = lax.all_to_all(row_normed, "lon", split_axis=0, concat_axis=0, tiled=True)
    home = antipode(to_home)
    third = third + late
    third_far = [swap_bands(piece) for piece in third]
    spread, home = lax.optimization_barrier((spread, home))
    sems = pltpu.SemaphoreType.DMA((2, lon_count))
    row_mixed = call(
        functools.partial(row_kernel, shard, cols, band // lon_count),
        bf16(tokens, 2 * attend),
        "row_attention",
        (place, row_slopes),
        (spread,),
        (*third, *third_far),
        [pltpu.VMEM((2, *project_shape.shape), jnp.bfloat16), sems],
        room=60,
    )
    back = lax.all_to_all(row_mixed, "lon", split_axis=0, concat_axis=0, tiled=True)
    given = (*third, *third_far, fields, mask, embed)
    middle, row_out = call(
        functools.partial(home_kernel, shard, lon_count),
        (f32(tokens, width), bf16(2, *output_shape.shape)),
        "middle",
        (place,),
        (mixed_own, theirs, home, output, output_far),
        given,
        [pltpu.VMEM(v.shape, v.dtype) for v in given[-3:]] + [sems, pltpu.SemaphoreType.DMA((3,))],
        room=56,
    )
    return call(
        final_kernel, bf16(band, cols, width), "block_output", (), (middle, back, row_out)
    )


def passed_along(value, axis, by):
    length = lax.axis_size(axis)
    return lax.ppermute(value, axis, [(i, (i + by) % length) for i in range(length)])


def layer_norm(values, gain):
    center = values - jnp.mean(values, axis=-1, keepdims=True)
    spread = jnp.mean(center * center, axis=-1, keepdims=True)
    return center * lax.rsqrt(spread + 1e-05) * gain


def unit_rms(vectors):
    return vectors * lax.rsqrt(jnp.mean(vectors * vectors, axis=-1, keepdims=True) + 1e-06)


def head_split(projected):
    query = unit_rms(projected[..., 0, :]).astype(jnp.bfloat16)
    keyed = unit_rms(projected[..., 1, :]).astype(jnp.bfloat16)
    valued = projected[..., 2, :].astype(jnp.bfloat16)
    return (query, keyed, valued)


def gather_bands(normed):
    return lax.all_gather(normed, "lat", axis=0, tiled=True)


def sum_heads(partial_value):
    return lax.psum_scatter(
        partial_value.astype(jnp.bfloat16), "lat", scatter_dimension=0, tiled=True
    ).astype(jnp.float32)


def project_in(normed, weight):
    return jnp.dot(
        normed,
        lax.all_gather(weight, "lon", axis=0, tiled=True),
        preferred_element_type=jnp.float32,
    )


def project_out(mixed, weight):
    return lax.dot_general(
        mixed,
        lax.all_gather(weight, "lon", axis=0, tiled=True),
        (((1,), (1,)), ((), ())),
        preferred_element_type=jnp.float32,
    )


def column_attend(query, column_kv, far_kv, slopes):
    total_rows = column_kv.shape[0]
    keyed = jnp.concatenate([column_kv[..., :HS], far_kv[..., :HS]], axis=0)
    valued = jnp.concatenate([column_kv[..., HS:], far_kv[..., HS:]], axis=0)
    scores = jnp.einsum("rchd,schd->chrs", query, keyed, preferred_element_type=jnp.float32)
    rows_here = jnp.arange(query.shape[0], dtype=jnp.int32)
    key_rows = jnp.arange(total_rows, dtype=jnp.int32)
    near_dist = jnp.abs(rows_here[:, None] - key_rows[None, :])
    pair_sum = rows_here[:, None] + key_rows[None, :]
    far_dist = jnp.minimum(pair_sum + 1, 2 * total_rows - 1 - pair_sum)
    distance = jnp.concatenate([near_dist, far_dist], axis=1).astype(jnp.float32)
    weight = jnp.exp(scores * (1.0 / math.sqrt(HS)) - slopes[None, :, None, None] * distance)
    prob = (weight / jnp.sum(weight, axis=-1, keepdims=True)).astype(jnp.bfloat16)
    mixed = jnp.einsum("chrs,schd->rchd", prob, valued, preferred_element_type=jnp.float32)
    return mixed.astype(jnp.bfloat16).reshape(query.shape[0], query.shape[1], -1)


def general(
    fields,
    land_mask,
    land_embed,
    column_gain,
    row_gain,
    column_slopes,
    row_slopes,
    column_project,
    column_output,
    row_project,
    row_output,
):
    lon_count = lax.axis_size("lon")
    lat_count = lax.axis_size("lat")
    band_rows, local_cols, width = fields.shape
    lat_place = lax.axis_index("lat")
    head_total = column_slopes.shape[0]
    head_share = head_total // lat_count
    first_head = lat_place * head_share
    start = fields.astype(jnp.float32) + land_mask.astype(jnp.float32)[..., None] * land_embed
    normed = layer_norm(start, column_gain).astype(jnp.bfloat16)
    whole = gather_bands(normed)
    projected = project_in(whole.reshape(-1, width), column_project)
    query, keyed, valued = head_split(
        projected.reshape(band_rows * lat_count, local_cols, head_share, 3, HS)
    )
    column_kv = jnp.concatenate([keyed, valued], axis=-1).reshape(
        band_rows * lat_count, local_cols, -1
    )
    slopes = lax.dynamic_slice_in_dim(column_slopes, first_head, head_share)
    far_kv = passed_along(column_kv, "lon", lon_count // 2)
    shaped = column_kv.shape[:2] + (head_share, 2 * HS)
    mixed = column_attend(query, column_kv.reshape(shaped), far_kv.reshape(shaped), slopes)
    partial_value = project_out(mixed.reshape(-1, head_share * HS), column_output)
    update = sum_heads(partial_value.reshape(band_rows * lat_count, local_cols, width))
    middle = start + update
    total_rows = band_rows * lat_count
    row_normed = layer_norm(middle, row_gain).astype(jnp.bfloat16)
    whole_rows = gather_bands(row_normed)
    projected = project_in(whole_rows.reshape(-1, width), row_project)
    query, keyed, valued = head_split(projected.reshape(total_rows, local_cols, head_share, 3, HS))
    packed = jnp.stack([query, keyed, valued], axis=3)
    parts = lax.all_to_all(packed, "lon", split_axis=0, concat_axis=1, tiled=True)
    few_rows, all_cols = (parts.shape[0], parts.shape[1])
    scores = jnp.einsum(
        "rchd,rehd->rhce", parts[..., 0, :], parts[..., 1, :], preferred_element_type=jnp.float32
    )
    cols_here = jnp.arange(all_cols, dtype=jnp.int32)
    gap = jnp.abs(cols_here[:, None] - cols_here[None, :])
    cycle_dist = jnp.minimum(gap, all_cols - gap).astype(jnp.float32)
    row_slope = lax.dynamic_slice_in_dim(row_slopes, first_head, head_share)
    weight = jnp.exp(scores * (1.0 / math.sqrt(HS)) - row_slope[None, :, None, None] * cycle_dist)
    prob = (weight / jnp.sum(weight, axis=-1, keepdims=True)).astype(jnp.bfloat16)
    row_mixed = jnp.einsum(
        "rhce,rehd->rchd", prob, parts[..., 2, :], preferred_element_type=jnp.float32
    )
    row_mixed = row_mixed.astype(jnp.bfloat16)
    back = lax.all_to_all(row_mixed, "lon", split_axis=1, concat_axis=0, tiled=True)
    partial_value = project_out(back.reshape(-1, head_share * HS), row_output)
    final_update = sum_heads(partial_value.reshape(total_rows, local_cols, width))
    return (middle + final_update).astype(jnp.bfloat16)


def solution(mesh):
    in_specs = (
        P("lat", "lon", None),
        P("lat", "lon"),
        P(),
        P(),
        P(),
        P(),
        P(),
        P("lon", "lat"),
        P("lon", "lat"),
        P("lon", "lat"),
        P("lon", "lat"),
    )
    out_specs = P(("ens", "lat"), "lon", None)

    def shards(fields, *rest):
        length = lax.axis_size("lon")
        suits = fields.shape[0] % length == 0 and length in (2 * PLANE, 4 * PLANE)
        return (fast if suits else general)(fields, *rest)

    return jax.shard_map(shards, mesh=mesh, in_specs=in_specs, out_specs=out_specs, check_vma=False)
```

```python
import functools
import math

import jax
import jax.numpy as jnp
from jax import lax
from jax.experimental import pallas as pl
from jax.experimental.pallas import tpu as pltpu
from jax.sharding import PartitionSpec as P

HS = 64
PAIR = 2 * HS
PLANE = 4
NEVER = -1e30
EXTRA = 16
CHUNKS = 4


def at(place, length):
    return [(i, place(i)) for i in range(length)]


def swap_bands(value):
    return lax.ppermute(value, "lat", at(lambda i: 1 - i, 2))


SCALARS = pl.BlockSpec(memory_space=pltpu.SMEM)


def call(
    kernel,
    out,
    name,
    arrays=(),
    scalars=(),
    given=(),
    scratch=(),
    cost=2**10,
    room=24,
    space=pltpu.VMEM,
):
    return pl.pallas_call(
        kernel,
        out_shape=out,
        in_specs=[SCALARS] * len(scalars)
        + [pl.BlockSpec(memory_space=pltpu.VMEM)] * len(arrays)
        + [pl.BlockSpec(memory_space=pltpu.HBM)] * len(given),
        out_specs=jax.tree.map(lambda _: pl.BlockSpec(memory_space=space), out),
        scratch_shapes=scratch,
        compiler_params=pltpu.CompilerParams(vmem_limit_bytes=room * 2**20),
        cost_estimate=pl.CostEstimate(flops=2**10, bytes_accessed=cost, transcendentals=0),
        name=name,
    )(*scalars, *arrays, *given)


def own_place():
    return lax.axis_index("lon"), lax.axis_index("lat")


def dot(a, b):
    return jnp.dot(a, b, preferred_element_type=jnp.float32)


def dot_t(a, b):
    return lax.dot_general(a, b, (((1,), (1,)), ((), ())), preferred_element_type=jnp.float32)


def iota(shape, axis):
    return lax.broadcasted_iota(jnp.int32, shape, axis)


def bring(pairs, sems):
    copies = [pltpu.make_async_copy(ref, held, sems.at[i]) for i, (ref, held) in enumerate(pairs)]
    for copy in copies:
        copy.start()
    return copies


def wait(copies):
    for copy in copies:
        copy.wait()


def along_lines(weight, length):
    steps = range(PLANE, length, PLANE)
    return [lax.ppermute(weight, "lon", at(lambda i: i ^ k, length)) for k in steps]


def doubled(weight, step, length):
    got = lax.ppermute(weight, "lon", at(lambda i: i ^ step, length))
    half = weight.shape[0] // 2
    return jnp.concatenate([weight[:half], got[:half], weight[half:], got[half:]], axis=0)


def across_plane(part, length):
    return [part] + [lax.ppermute(part, "lon", at(lambda i: i ^ k, length)) for k in range(1, PLANE)]


def relayed_plane(part, length):
    half = part.shape[0] // 2
    step = lambda value, k: lax.ppermute(value, "lon", at(lambda i: i ^ k, length))
    first, second = step(part, 1), step(part, 2)
    return [part, first, second], [step(second[:half], 1), step(first[half:], 2)]


def by_kind(weight):
    heads = weight.shape[1] // (3 * HS)
    block = lambda kind, head: weight[:, (3 * head + kind) * HS : (3 * head + kind + 1) * HS]
    return jnp.concatenate([block(kind, head) for kind in range(3) for head in range(heads)], axis=1)


def places(shard, place, pieces):
    line, spot = place[0] // PLANE, place[0] % PLANE
    lines = pieces[0].shape[0] // shard
    blocks = [(piece, k) for piece in pieces for k in range(piece.shape[0] // shard)]
    for number, (piece, k) in enumerate(blocks):
        owner = lax.bitwise_xor(line, number % lines) * PLANE
        owner += lax.bitwise_xor(spot, number // lines)
        there = pl.ds(pl.multiple_of(owner * shard, shard), shard)
        yield piece, slice(k * shard, (k + 1) * shard), there


def order_kernel(shard, sort, w0, w1, w2, w3, out):
    place = own_place()
    for piece, here, there in places(shard, place, (w0, w1, w2, w3)):
        out[there, :] = by_kind(piece[here, :]) if sort else piece[here, :]


def bring_in_order(shard, place, pieces, lane, target, sems):
    lanes = slice(lane, lane + target.shape[1])
    return bring(
        [
            (piece.at[here, lanes], target.at[there, :])
            for piece, here, there in places(shard, place, pieces)
        ],
        sems,
    )


def norm(values, gain):
    center = values - jnp.mean(values, axis=-1, keepdims=True)
    spread = jnp.mean(center * center, axis=-1, keepdims=True)
    return center * lax.rsqrt(spread + 1e-05) * gain


def land_start(tokens, mask, embed):
    cols, rows = mask.shape
    total = rows * cols
    row_of = (iota((total, rows), 0) // cols == iota((total, rows), 1)).astype(jnp.bfloat16)
    spread = dot_t(row_of, mask.astype(jnp.bfloat16))
    own = iota((total, cols), 0) % cols == iota((total, cols), 1)
    land = jnp.sum(jnp.where(own, spread, 0.0), axis=1, keepdims=True)
    return tokens.astype(jnp.float32).reshape(total, tokens.shape[2]) + land * embed


def packed_start(packed, embed):
    total = packed.shape[0] - EXTRA
    row = packed[total : total + 1, :total].astype(jnp.float32)
    same = iota((total, total), 0) == iota((total, total), 1)
    land = jnp.sum(jnp.where(same, row, 0.0), axis=1, keepdims=True)
    return packed[:total, :].astype(jnp.float32) + land * embed


def slots(cols, rows, side, inverse=False):
    total = cols * rows
    spot, grid = iota((total, total), int(inverse)), iota((total, total), int(not inverse))
    column = lax.rem(spot // rows + side * (cols // 2), cols)
    return (grid == lax.rem(spot, rows) * cols + column).astype(jnp.bfloat16)


def first_kernel(lons, tokens, mask, project, output, keep, send, packed, *scratch):
    place = own_place()
    *held, sems = scratch
    coming = bring(zip((tokens, mask, project, output), held), sems)
    tokens, mask, project, output = held
    rows, cols, width = tokens.shape
    half = rows * cols // 2
    side = place[0] // (lons // 2)
    to_slots = slots(cols, rows, side)
    wait(coming[:2])
    flat = tokens[...].astype(jnp.float32).reshape(rows * cols, width).astype(jnp.bfloat16)
    in_slots = dot(to_slots, flat).astype(jnp.bfloat16)
    land = mask[...].astype(jnp.float32)
    parts = [land[c : c + 1, :] for c in range(cols)]
    halves = [jnp.concatenate(parts[: cols // 2], axis=1), jnp.concatenate(parts[cols // 2 :], axis=1)]
    for k, out in enumerate((keep, send)):
        out[:half, :] = in_slots[k * half : (k + 1) * half]
        out[half:, :] = jnp.zeros((EXTRA, width), jnp.bfloat16)
        row = jnp.where(side == k, halves[0], halves[1])
        out[half:, :half] = jnp.broadcast_to(row, (EXTRA, half)).astype(jnp.bfloat16)
    wait(coming[2:])
    split = project.shape[1]
    packed[:, :split] = by_kind(project[...])
    packed[:, split:] = output[...]


def column_norm_kernel(own, other, embed, gain, out):
    half = own.shape[0] - EXTRA
    for k, ref in enumerate((own, other)):
        normed = norm(packed_start(ref[...], embed[...]), gain[...])
        out[k * half : (k + 1) * half, :] = normed.astype(jnp.bfloat16)


def unit_heads(vectors, scale=1.0):
    width = vectors.shape[1]
    same = (iota((width, width), 0) // HS == iota((width, width), 1) // HS).astype(jnp.bfloat16)
    total = dot((vectors * vectors).astype(jnp.bfloat16), same)
    return (vectors * (lax.rsqrt(total * (1.0 / HS) + 1e-06) * scale)).astype(jnp.bfloat16)


def two_heads(query, keyed, valued, bias):
    rows = query.shape[0]
    first = iota(query.shape, 1) < HS
    zero = jnp.zeros_like(query)
    stacked = jnp.concatenate([jnp.where(first, query, zero), jnp.where(first, zero, query)], axis=0)
    weight = jnp.exp(dot_t(stacked, keyed) + bias).astype(jnp.bfloat16)
    widened = jnp.concatenate([valued, jnp.ones_like(valued)], axis=1)
    mixed = dot(weight, widened)
    mixed = mixed[:, :PAIR] / mixed[:, PAIR:]
    return jnp.where(first, mixed[:rows], mixed[rows:]).astype(jnp.bfloat16)


def column_kernel(band, slopes, tokens, far_tokens, weight, out_own, out_other, qkv):
    place = own_place()
    block = tokens.shape[0] // 2
    loops = block // band
    width = weight.shape[1] // 3
    for half, ref in enumerate((tokens, far_tokens)):
        projected = dot(ref[...], weight[...])
        at_rows = slice(half * 2 * block, (half + 1) * 2 * block)
        qkv[at_rows, :width] = unit_heads(projected[:, :width], 1.0 / math.sqrt(HS))
        qkv[at_rows, width : 2 * width] = unit_heads(projected[:, width : 2 * width])
        qkv[at_rows, 2 * width :] = projected[:, 2 * width :].astype(jnp.bfloat16)
    total = 2 * band
    shape = (2 * total, 2 * total)
    spot_q, spot_k = iota(shape, 0), iota(shape, 1)
    shift = place[1] * band
    row_q, row_k = lax.rem(spot_q + shift, total), lax.rem(spot_k + shift, total)
    pair_sum = row_q + row_k
    beyond = jnp.minimum(pair_sum + 1, 2 * total - 1 - pair_sum)
    here = (spot_q < total) == (spot_k < total)
    distance = jnp.where(here, jnp.abs(row_q - row_k), beyond).astype(jnp.float32)
    first = place[1] * (width // HS)
    for pair in range(width // PAIR):
        bias = jnp.concatenate(
            [distance * -slopes[first + 2 * pair + one] for one in range(2)], axis=0
        )
        lanes = slice(pair * PAIR, (pair + 1) * PAIR)
        for loop in range(loops):
            starts = [part * block + loop * band for part in range(4)]
            query, keyed, valued = (
                jnp.concatenate(
                    [
                        qkv[at : at + band, kind * width + lanes.start : kind * width + lanes.stop]
                        for at in starts
                    ],
                    axis=0,
                )
                for kind in range(3)
            )
            mixed = two_heads(query, keyed, valued, bias)
            for part in range(4):
                out = (out_own, out_other)[part % 2]
                slot = (part // 2) * loops + loop
                out[slot * band : (slot + 1) * band, lanes] = mixed[part * band : (part + 1) * band]


def middle_kernel(cols, mine, theirs, near, far, kept, got, embed, gain, out):
    update = dot_t(mine[...], near[...]) + dot_t(theirs[...], far[...])
    parts = [packed_start(ref[...], embed[...]) for ref in (kept, got)]
    middle = jnp.concatenate(parts, axis=0) + update
    normed = norm(middle, gain[...]).astype(jnp.bfloat16)
    by_row = slots(cols, normed.shape[0] // cols, 0, True)
    out[...] = dot(by_row, normed).astype(jnp.bfloat16)


def home_kernel(shard, lons, mine, theirs, back, near, far, *refs):
    place = own_place()
    pieces, (tokens, mask, embed, out, out_weight, *held, weight_sems, sems) = refs[:-10], refs[-10:]
    lane = pieces[0].shape[1] - out_weight.shape[2]
    coming = bring(zip((tokens, mask, embed), held), sems)
    count = len(pieces) // 2
    later = []
    for half in range(2):
        mine_of = pieces[half * count : (half + 1) * count]
        later += bring_in_order(shard, place, mine_of, lane, out_weight.at[half], weight_sems.at[half])
    tokens, mask, embed = held
    rows, cols, _ = tokens.shape
    half, width = rows * cols // 2, near.shape[1]
    to_grid = slots(cols, rows, place[0] // (lons // 2), True)
    update = 0.0
    for lane, (kept, weight) in enumerate(((mine, near), (theirs, far))):
        mixed = dot(to_grid[:, :half], kept[:half, :])
        mixed += dot(to_grid[:, half:], back[:, lane * width : (lane + 1) * width])
        update += dot_t(mixed.astype(jnp.bfloat16), weight[...])
    wait(coming)
    out[...] = land_start(tokens[...], mask[...], embed[...]) + update
    wait(later)


def row_kernel(shard, cols, rows, slopes, spread, *refs):
    place = own_place()
    pieces, (out, tokens, weight, sems, token_sem) = refs[:-5], refs[-5:]
    count = len(pieces) // 2
    fetch = lambda half: bring_in_order(
        shard, place, pieces[half * count : (half + 1) * count], 0, weight.at[half], sems.at[half]
    )
    first_copy = bring([(spread, tokens)], token_sem)
    coming = fetch(0)
    wait(first_copy)
    total = tokens.shape[0]
    block = cols * rows
    lon_count = total // block
    circle = lon_count * cols
    turn, part = lon_count // 2, cols // 2
    spot_q, spot_k = iota((total, total), 0), iota((total, total), 1)

    def lon_of(spot):
        device, slot = spot // block, lax.rem(spot, cols)
        side = device // turn
        holder = lax.rem(device + (slot // part) * turn, lon_count)
        return holder * cols + side * part + lax.rem(slot, part)

    row_of = lambda spot: lax.rem(spot, block) // cols
    gap = jnp.abs(lon_of(spot_q) - lon_of(spot_k))
    distance = jnp.minimum(gap, circle - gap).astype(jnp.float32)
    column = lax.rem(spot_q, cols)
    away = (column // part != spot_q // block // turn).astype(jnp.int32)
    home = lax.rem(spot_q // block + away * turn, lon_count) * block
    home = home + row_of(spot_q) * cols + away * part + lax.rem(column, part)
    homeward = (spot_k == home).astype(jnp.bfloat16)
    same = row_of(spot_q) == row_of(spot_k)
    width = weight.shape[2] // 3
    heads = width // HS
    for half in range(2):
        first = lax.rem(place[1] + half, 2) * heads
        wait(coming)
        if half == 0:
            coming = fetch(1)
        projected = dot(tokens[...], weight[half])
        query = unit_heads(projected[:, :width], 1.0 / math.sqrt(HS))
        keyed = unit_heads(projected[:, width : 2 * width])
        valued = projected[:, 2 * width :].astype(jnp.bfloat16)
        for pair in range(width // PAIR):
            lanes = slice(pair * PAIR, (pair + 1) * PAIR)
            bias = jnp.concatenate(
                [
                    jnp.where(same, distance * -slopes[first + 2 * pair + one], NEVER)
                    for one in range(2)
                ],
                axis=0,
            )
            mixed = two_heads(query[:, lanes], keyed[:, lanes], valued[:, lanes], bias)
            start = half * width + pair * PAIR
            out[:, start : start + PAIR] = dot(homeward, mixed).astype(jnp.bfloat16)


def final_kernel(mixed, middle, weight, out, mixed_held, total, held, staged, sems, out_sems):
    width = held.shape[2]
    step = total.shape[1] // CHUNKS
    cut = [slice(i * step, (i + 1) * step) for i in range(CHUNKS)]
    pairs = [(mixed, mixed_held)]
    for at_cols in cut:
        pairs += [(weight.at[half, at_cols, :], held.at[half, at_cols, :]) for half in range(2)]
        pairs += [(middle.at[:, at_cols], total.at[:, at_cols])]
    coming = bring(pairs, sems)
    coming[0].wait()
    going = []
    for i, at_cols in enumerate(cut):
        wait(coming[1 + 3 * i : 4 + 3 * i])
        update = total[:, at_cols]
        for half in range(2):
            update += dot_t(mixed_held[:, half * width : (half + 1) * width], held[half, at_cols, :])
        staged[:, :, at_cols] = update.reshape(*out.shape[:2], step).astype(jnp.bfloat16)
        copy = pltpu.make_async_copy(staged.at[:, :, at_cols], out.at[:, :, at_cols], out_sems.at[i])
        copy.start()
        going.append(copy)
    wait(going)


def fast(
    fields,
    land_mask,
    land_embed,
    column_gain,
    row_gain,
    column_slopes,
    row_slopes,
    column_project,
    column_output,
    row_project,
    row_output,
):
    lon_count = lax.axis_size("lon")
    band, cols, width = fields.shape
    tokens = band * cols
    attend = column_slopes.shape[0] // 2 * HS
    shard = column_project.shape[0]
    embed, column_gain, row_gain = (v.reshape(1, width) for v in (land_embed, column_gain, row_gain))
    mask = land_mask.T
    bf16 = lambda *shape: jax.ShapeDtypeStruct(shape, jnp.bfloat16)
    f32 = lambda *shape: jax.ShapeDtypeStruct(shape, jnp.float32)
    vmem = lambda *arrays: [pltpu.VMEM(v.shape, v.dtype) for v in arrays]
    sems = lambda *shape: [pltpu.SemaphoreType.DMA(shape)]
    after = lax.optimization_barrier
    project_shape = bf16(shard * lon_count, 3 * attend)
    output_shape = bf16(shard * lon_count, attend)
    antipode = lambda value: lax.ppermute(
        value, "lon", at(lambda i: (i + lon_count // 2) % lon_count, lon_count)
    )
    two_lines = lambda value: lax.ppermute(value, "lon", at(lambda i: i ^ (2 * PLANE), lon_count))

    given = (fields, mask, row_project, row_output)
    packed = bf16(tokens // 2 + EXTRA, width)
    keep, send, row_weights = call(
        functools.partial(first_kernel, lon_count),
        (packed, packed, bf16(shard, 4 * attend)),
        "loop_tokens",
        given=given,
        scratch=vmem(*given) + sems(4),
        room=60,
    )
    lines = along_lines(column_project, lon_count)
    output_got, row_got = two_lines(column_output), two_lines(row_weights)
    keep_other = swap_bands(keep)
    *lines, send = after((*lines, send))
    far = antipode(send)
    project = jnp.concatenate([column_project, *lines], axis=0)
    output = jnp.concatenate([column_output, output_got], axis=0)
    row_weights = jnp.concatenate([row_weights, row_got], axis=0)
    project, keep_other = after((project, keep_other))
    project = across_plane(project, lon_count)
    output = doubled(output, PLANE, lon_count)
    far_other = swap_bands(far)

    column_normed = lambda own, other, name: call(
        column_norm_kernel, bf16(tokens, width), name, (own, other, embed, column_gain)
    )
    kept_normed = column_normed(keep, keep_other, "column_normed")
    far_normed = column_normed(far, far_other, "far_normed")
    project = call(
        functools.partial(order_kernel, shard, True), project_shape, "column_project", project
    )
    far_normed, project, output = after((far_normed, project, output))
    row_weights, _ = after((row_weights, far))
    output = across_plane(output, lon_count)
    row_weights = doubled(row_weights, PLANE, lon_count)
    mixed_own, mixed_other = call(
        functools.partial(column_kernel, band),
        (bf16(tokens, attend), bf16(tokens, attend)),
        "column_attention",
        (kept_normed, far_normed, project),
        scalars=(column_slopes,),
        scratch=[pltpu.VMEM((2 * tokens, 3 * attend), jnp.bfloat16)],
        cost=2**18,
    )
    theirs = swap_bands(mixed_other)
    output, row_weights, mixed_own = after((output, row_weights, mixed_own))
    output = call(functools.partial(order_kernel, shard, False), output_shape, "column_output", output)
    output_far = swap_bands(output)

    to_home = jnp.concatenate([mixed_own[tokens // 2 :], theirs[tokens // 2 :]], axis=1)
    row_weights, late = relayed_plane(row_weights, lon_count)
    row_normed = call(
        functools.partial(middle_kernel, cols),
        bf16(tokens, width),
        "row_normed",
        (mixed_own, theirs, output, output_far, keep, far, embed, row_gain),
    )
    spread = lax.all_to_all(row_normed, "lon", split_axis=0, concat_axis=0, tiled=True)
    to_home, row_weights = after((to_home, row_weights))
    home = antipode(to_home)
    row_weights = row_weights + late
    row_weights += [swap_bands(piece) for piece in row_weights]

    row_mixed = call(
        functools.partial(row_kernel, shard, cols, band // lon_count),
        bf16(tokens, 2 * attend),
        "row_attention",
        scalars=(row_slopes,),
        given=(spread, *row_weights),
        scratch=vmem(spread.reshape(tokens, width))
        + [pltpu.VMEM((2, *project_shape.shape), jnp.bfloat16)]
        + sems(2, lon_count)
        + sems(1),
        room=60,
    )
    row_mixed, home = after((row_mixed, home))
    back = lax.all_to_all(row_mixed, "lon", split_axis=0, concat_axis=0, tiled=True)
    given = (fields, mask, embed)
    middle, row_out = call(
        functools.partial(home_kernel, shard, lon_count),
        (f32(tokens, width), bf16(2, *output_shape.shape)),
        "middle",
        (mixed_own, theirs, home, output, output_far),
        given=(*row_weights, *given),
        scratch=vmem(*given) + sems(2, lon_count) + sems(3),
        room=56,
    )
    return call(
        final_kernel,
        bf16(band, cols, width),
        "block_output",
        given=(back, middle, row_out),
        scratch=vmem(back, middle, row_out)
        + [pltpu.VMEM(fields.shape, jnp.bfloat16)]
        + sems(1 + 3 * CHUNKS)
        + sems(CHUNKS),
        room=60,
        space=pltpu.HBM,
    )


def passed_along(value, axis, by):
    length = lax.axis_size(axis)
    return lax.ppermute(value, axis, [(i, (i + by) % length) for i in range(length)])


def layer_norm(values, gain):
    center = values - jnp.mean(values, axis=-1, keepdims=True)
    spread = jnp.mean(center * center, axis=-1, keepdims=True)
    return center * lax.rsqrt(spread + 1e-05) * gain


def unit_rms(vectors):
    return vectors * lax.rsqrt(jnp.mean(vectors * vectors, axis=-1, keepdims=True) + 1e-06)


def head_split(projected):
    query = unit_rms(projected[..., 0, :]).astype(jnp.bfloat16)
    keyed = unit_rms(projected[..., 1, :]).astype(jnp.bfloat16)
    valued = projected[..., 2, :].astype(jnp.bfloat16)
    return (query, keyed, valued)


def gather_bands(normed):
    return lax.all_gather(normed, "lat", axis=0, tiled=True)


def sum_heads(partial_value):
    return lax.psum_scatter(
        partial_value.astype(jnp.bfloat16), "lat", scatter_dimension=0, tiled=True
    ).astype(jnp.float32)


def project_in(normed, weight):
    return jnp.dot(
        normed,
        lax.all_gather(weight, "lon", axis=0, tiled=True),
        preferred_element_type=jnp.float32,
    )


def project_out(mixed, weight):
    return lax.dot_general(
        mixed,
        lax.all_gather(weight, "lon", axis=0, tiled=True),
        (((1,), (1,)), ((), ())),
        preferred_element_type=jnp.float32,
    )


def column_attend(query, column_kv, far_kv, slopes):
    total_rows = column_kv.shape[0]
    keyed = jnp.concatenate([column_kv[..., :HS], far_kv[..., :HS]], axis=0)
    valued = jnp.concatenate([column_kv[..., HS:], far_kv[..., HS:]], axis=0)
    scores = jnp.einsum("rchd,schd->chrs", query, keyed, preferred_element_type=jnp.float32)
    rows_here = jnp.arange(query.shape[0], dtype=jnp.int32)
    key_rows = jnp.arange(total_rows, dtype=jnp.int32)
    near_dist = jnp.abs(rows_here[:, None] - key_rows[None, :])
    pair_sum = rows_here[:, None] + key_rows[None, :]
    far_dist = jnp.minimum(pair_sum + 1, 2 * total_rows - 1 - pair_sum)
    distance = jnp.concatenate([near_dist, far_dist], axis=1).astype(jnp.float32)
    weight = jnp.exp(scores * (1.0 / math.sqrt(HS)) - slopes[None, :, None, None] * distance)
    prob = (weight / jnp.sum(weight, axis=-1, keepdims=True)).astype(jnp.bfloat16)
    mixed = jnp.einsum("chrs,schd->rchd", prob, valued, preferred_element_type=jnp.float32)
    return mixed.astype(jnp.bfloat16).reshape(query.shape[0], query.shape[1], -1)


def general(
    fields,
    land_mask,
    land_embed,
    column_gain,
    row_gain,
    column_slopes,
    row_slopes,
    column_project,
    column_output,
    row_project,
    row_output,
):
    lon_count = lax.axis_size("lon")
    lat_count = lax.axis_size("lat")
    band_rows, local_cols, width = fields.shape
    lat_place = lax.axis_index("lat")
    head_total = column_slopes.shape[0]
    head_share = head_total // lat_count
    first_head = lat_place * head_share
    start = fields.astype(jnp.float32) + land_mask.astype(jnp.float32)[..., None] * land_embed
    normed = layer_norm(start, column_gain).astype(jnp.bfloat16)
    whole = gather_bands(normed)
    projected = project_in(whole.reshape(-1, width), column_project)
    query, keyed, valued = head_split(
        projected.reshape(band_rows * lat_count, local_cols, head_share, 3, HS)
    )
    column_kv = jnp.concatenate([keyed, valued], axis=-1).reshape(
        band_rows * lat_count, local_cols, -1
    )
    slopes = lax.dynamic_slice_in_dim(column_slopes, first_head, head_share)
    far_kv = passed_along(column_kv, "lon", lon_count // 2)
    shaped = column_kv.shape[:2] + (head_share, 2 * HS)
    mixed = column_attend(query, column_kv.reshape(shaped), far_kv.reshape(shaped), slopes)
    partial_value = project_out(mixed.reshape(-1, head_share * HS), column_output)
    update = sum_heads(partial_value.reshape(band_rows * lat_count, local_cols, width))
    middle = start + update
    total_rows = band_rows * lat_count
    row_normed = layer_norm(middle, row_gain).astype(jnp.bfloat16)
    whole_rows = gather_bands(row_normed)
    projected = project_in(whole_rows.reshape(-1, width), row_project)
    query, keyed, valued = head_split(projected.reshape(total_rows, local_cols, head_share, 3, HS))
    packed = jnp.stack([query, keyed, valued], axis=3)
    parts = lax.all_to_all(packed, "lon", split_axis=0, concat_axis=1, tiled=True)
    few_rows, all_cols = (parts.shape[0], parts.shape[1])
    scores = jnp.einsum(
        "rchd,rehd->rhce", parts[..., 0, :], parts[..., 1, :], preferred_element_type=jnp.float32
    )
    cols_here = jnp.arange(all_cols, dtype=jnp.int32)
    gap = jnp.abs(cols_here[:, None] - cols_here[None, :])
    cycle_dist = jnp.minimum(gap, all_cols - gap).astype(jnp.float32)
    row_slope = lax.dynamic_slice_in_dim(row_slopes, first_head, head_share)
    weight = jnp.exp(scores * (1.0 / math.sqrt(HS)) - row_slope[None, :, None, None] * cycle_dist)
    prob = (weight / jnp.sum(weight, axis=-1, keepdims=True)).astype(jnp.bfloat16)
    row_mixed = jnp.einsum(
        "rhce,rehd->rchd", prob, parts[..., 2, :], preferred_element_type=jnp.float32
    )
    row_mixed = row_mixed.astype(jnp.bfloat16)
    back = lax.all_to_all(row_mixed, "lon", split_axis=1, concat_axis=0, tiled=True)
    partial_value = project_out(back.reshape(-1, head_share * HS), row_output)
    final_update = sum_heads(partial_value.reshape(total_rows, local_cols, width))
    return (middle + final_update).astype(jnp.bfloat16)


def solution(mesh):
    in_specs = (
        P("lat", "lon", None),
        P("lat", "lon"),
        P(),
        P(),
        P(),
        P(),
        P(),
        P("lon", "lat"),
        P("lon", "lat"),
        P("lon", "lat"),
        P("lon", "lat"),
    )
    out_specs = P(("ens", "lat"), "lon", None)

    def shards(fields, *rest):
        length = lax.axis_size("lon")
        suits = fields.shape[0] % length == 0 and length == 4 * PLANE
        return (fast if suits else general)(fields, *rest)

    return jax.shard_map(shards, mesh=mesh, in_specs=in_specs, out_specs=out_specs, check_vma=False)
```

```python
import functools
import math

import jax
import jax.numpy as jnp
from jax import lax
from jax.experimental import pallas as pl
from jax.experimental.pallas import tpu as pltpu
from jax.sharding import PartitionSpec as P

HS = 64
PAIR = 2 * HS
PLANE = 4
NEVER = -1e30
EXTRA = 16


def at(place, length):
    return [(i, place(i)) for i in range(length)]


def swap_bands(value):
    return lax.ppermute(value, "lat", at(lambda i: 1 - i, 2))


SCALARS = pl.BlockSpec(memory_space=pltpu.SMEM)


def call(
    kernel,
    out,
    name,
    arrays=(),
    scalars=(),
    given=(),
    scratch=(),
    cost=2**10,
    room=24,
    space=pltpu.VMEM,
):
    return pl.pallas_call(
        kernel,
        out_shape=out,
        in_specs=[SCALARS] * len(scalars)
        + [pl.BlockSpec(memory_space=pltpu.VMEM)] * len(arrays)
        + [pl.BlockSpec(memory_space=pltpu.HBM)] * len(given),
        out_specs=jax.tree.map(lambda _: pl.BlockSpec(memory_space=space), out),
        scratch_shapes=scratch,
        compiler_params=pltpu.CompilerParams(vmem_limit_bytes=room * 2**20),
        cost_estimate=pl.CostEstimate(flops=2**10, bytes_accessed=cost, transcendentals=0),
        name=name,
    )(*scalars, *arrays, *given)


def own_place():
    return lax.axis_index("lon"), lax.axis_index("lat")


def dot(a, b):
    return jnp.dot(a, b, preferred_element_type=jnp.float32)


def dot_t(a, b):
    return lax.dot_general(a, b, (((1,), (1,)), ((), ())), preferred_element_type=jnp.float32)


def iota(shape, axis):
    return lax.broadcasted_iota(jnp.int32, shape, axis)


def bring(pairs, sems):
    copies = [pltpu.make_async_copy(ref, held, sems.at[i]) for i, (ref, held) in enumerate(pairs)]
    for copy in copies:
        copy.start()
    return copies


def wait(copies):
    for copy in copies:
        copy.wait()


def along_lines(weight, length):
    steps = range(PLANE, length, PLANE)
    return [lax.ppermute(weight, "lon", at(lambda i: i ^ k, length)) for k in steps]


def doubled(weight, step, length):
    got = lax.ppermute(weight, "lon", at(lambda i: i ^ step, length))
    half = weight.shape[0] // 2
    return jnp.concatenate([weight[:half], got[:half], weight[half:], got[half:]], axis=0)


def across_plane(part, length):
    return [part] + [lax.ppermute(part, "lon", at(lambda i: i ^ k, length)) for k in range(1, PLANE)]


def relayed_plane(part, length):
    half = part.shape[0] // 2
    step = lambda value, k: lax.ppermute(value, "lon", at(lambda i: i ^ k, length))
    first, second = step(part, 1), step(part, 2)
    return [part, first, second], [step(second[:half], 1), step(first[half:], 2)]


def by_kind(weight):
    heads = weight.shape[1] // (3 * HS)
    block = lambda kind, head: weight[:, (3 * head + kind) * HS : (3 * head + kind + 1) * HS]
    return jnp.concatenate([block(kind, head) for kind in range(3) for head in range(heads)], axis=1)


def places(shard, place, pieces):
    line, spot = place[0] // PLANE, place[0] % PLANE
    lines = pieces[0].shape[0] // shard
    blocks = [(piece, k) for piece in pieces for k in range(piece.shape[0] // shard)]
    for number, (piece, k) in enumerate(blocks):
        owner = lax.bitwise_xor(line, number % lines) * PLANE
        owner += lax.bitwise_xor(spot, number // lines)
        there = pl.ds(pl.multiple_of(owner * shard, shard), shard)
        yield piece, slice(k * shard, (k + 1) * shard), there


def order_kernel(shard, sort, w0, w1, w2, w3, out):
    place = own_place()
    for piece, here, there in places(shard, place, (w0, w1, w2, w3)):
        out[there, :] = by_kind(piece[here, :]) if sort else piece[here, :]


def bring_in_order(shard, place, pieces, lane, target, sems):
    lanes = slice(lane, lane + target.shape[1])
    return bring(
        [
            (piece.at[here, lanes], target.at[there, :])
            for piece, here, there in places(shard, place, pieces)
        ],
        sems,
    )


def norm(values, gain):
    center = values - jnp.mean(values, axis=-1, keepdims=True)
    spread = jnp.mean(center * center, axis=-1, keepdims=True)
    return center * lax.rsqrt(spread + 1e-05) * gain


def land_start(tokens, mask, embed):
    cols, rows = mask.shape
    total = rows * cols
    row_of = (iota((total, rows), 0) // cols == iota((total, rows), 1)).astype(jnp.bfloat16)
    spread = dot_t(row_of, mask.astype(jnp.bfloat16))
    own = iota((total, cols), 0) % cols == iota((total, cols), 1)
    land = jnp.sum(jnp.where(own, spread, 0.0), axis=1, keepdims=True)
    return tokens.astype(jnp.float32).reshape(total, tokens.shape[2]) + land * embed


def packed_start(packed, embed):
    total = packed.shape[0] - EXTRA
    row = packed[total : total + 1, :total].astype(jnp.float32)
    same = iota((total, total), 0) == iota((total, total), 1)
    land = jnp.sum(jnp.where(same, row, 0.0), axis=1, keepdims=True)
    return packed[:total, :].astype(jnp.float32) + land * embed


def slots(cols, rows, side, inverse=False):
    total = cols * rows
    spot, grid = iota((total, total), int(inverse)), iota((total, total), int(not inverse))
    column = lax.rem(spot // rows + side * (cols // 2), cols)
    return (grid == lax.rem(spot, rows) * cols + column).astype(jnp.bfloat16)


def first_kernel(lons, tokens, mask, project, output, keep, send, packed, *scratch):
    place = own_place()
    *held, sems = scratch
    coming = bring(zip((tokens, mask, project, output), held), sems)
    tokens, mask, project, output = held
    rows, cols, width = tokens.shape
    half = rows * cols // 2
    side = place[0] // (lons // 2)
    to_slots = slots(cols, rows, side)
    wait(coming[:2])
    flat = tokens[...].astype(jnp.float32).reshape(rows * cols, width).astype(jnp.bfloat16)
    in_slots = dot(to_slots, flat).astype(jnp.bfloat16)
    land = mask[...].astype(jnp.float32)
    parts = [land[c : c + 1, :] for c in range(cols)]
    halves = [jnp.concatenate(parts[: cols // 2], axis=1), jnp.concatenate(parts[cols // 2 :], axis=1)]
    for k, out in enumerate((keep, send)):
        out[:half, :] = in_slots[k * half : (k + 1) * half]
        out[half:, :] = jnp.zeros((EXTRA, width), jnp.bfloat16)
        row = jnp.where(side == k, halves[0], halves[1])
        out[half:, :half] = jnp.broadcast_to(row, (EXTRA, half)).astype(jnp.bfloat16)
    wait(coming[2:])
    split = project.shape[1]
    packed[:, :split] = by_kind(project[...])
    packed[:, split:] = output[...]


def column_norm_kernel(own, other, embed, gain, out):
    half = own.shape[0] - EXTRA
    for k, ref in enumerate((own, other)):
        normed = norm(packed_start(ref[...], embed[...]), gain[...])
        out[k * half : (k + 1) * half, :] = normed.astype(jnp.bfloat16)


def unit_heads(vectors, scale=1.0):
    width = vectors.shape[1]
    same = (iota((width, width), 0) // HS == iota((width, width), 1) // HS).astype(jnp.bfloat16)
    total = dot((vectors * vectors).astype(jnp.bfloat16), same)
    return (vectors * (lax.rsqrt(total * (1.0 / HS) + 1e-06) * scale)).astype(jnp.bfloat16)


def two_heads(query, keyed, valued, bias):
    rows = query.shape[0]
    first = iota(query.shape, 1) < HS
    zero = jnp.zeros_like(query)
    stacked = jnp.concatenate([jnp.where(first, query, zero), jnp.where(first, zero, query)], axis=0)
    weight = jnp.exp(dot_t(stacked, keyed) + bias).astype(jnp.bfloat16)
    widened = jnp.concatenate([valued, jnp.ones_like(valued)], axis=1)
    mixed = dot(weight, widened)
    mixed = mixed[:, :PAIR] / mixed[:, PAIR:]
    return jnp.where(first, mixed[:rows], mixed[rows:]).astype(jnp.bfloat16)


def column_kernel(band, slopes, tokens, far_tokens, weight, out_own, out_other, qkv):
    place = own_place()
    block = tokens.shape[0] // 2
    loops = block // band
    width = weight.shape[1] // 3
    for half, ref in enumerate((tokens, far_tokens)):
        projected = dot(ref[...], weight[...])
        at_rows = slice(half * 2 * block, (half + 1) * 2 * block)
        qkv[at_rows, :width] = unit_heads(projected[:, :width], 1.0 / math.sqrt(HS))
        qkv[at_rows, width : 2 * width] = unit_heads(projected[:, width : 2 * width])
        qkv[at_rows, 2 * width :] = projected[:, 2 * width :].astype(jnp.bfloat16)
    total = 2 * band
    shape = (2 * total, 2 * total)
    spot_q, spot_k = iota(shape, 0), iota(shape, 1)
    shift = place[1] * band
    row_q, row_k = lax.rem(spot_q + shift, total), lax.rem(spot_k + shift, total)
    pair_sum = row_q + row_k
    beyond = jnp.minimum(pair_sum + 1, 2 * total - 1 - pair_sum)
    here = (spot_q < total) == (spot_k < total)
    distance = jnp.where(here, jnp.abs(row_q - row_k), beyond).astype(jnp.float32)
    first = place[1] * (width // HS)
    for pair in range(width // PAIR):
        bias = jnp.concatenate(
            [distance * -slopes[first + 2 * pair + one] for one in range(2)], axis=0
        )
        lanes = slice(pair * PAIR, (pair + 1) * PAIR)
        for loop in range(loops):
            starts = [part * block + loop * band for part in range(4)]
            query, keyed, valued = (
                jnp.concatenate(
                    [
                        qkv[at : at + band, kind * width + lanes.start : kind * width + lanes.stop]
                        for at in starts
                    ],
                    axis=0,
                )
                for kind in range(3)
            )
            mixed = two_heads(query, keyed, valued, bias)
            for part in range(4):
                out = (out_own, out_other)[part % 2]
                slot = (part // 2) * loops + loop
                out[slot * band : (slot + 1) * band, lanes] = mixed[part * band : (part + 1) * band]


def middle_kernel(cols, mine, theirs, near, far, kept, got, embed, gain, out):
    update = dot_t(mine[...], near[...]) + dot_t(theirs[...], far[...])
    parts = [packed_start(ref[...], embed[...]) for ref in (kept, got)]
    middle = jnp.concatenate(parts, axis=0) + update
    normed = norm(middle, gain[...]).astype(jnp.bfloat16)
    by_row = slots(cols, normed.shape[0] // cols, 0, True)
    out[...] = dot(by_row, normed).astype(jnp.bfloat16)


def home_kernel(shard, lons, mine, theirs, back, near, far, *refs):
    place = own_place()
    pieces, (tokens, mask, embed, out, out_weight, *held, weight_sems, sems) = refs[:-10], refs[-10:]
    lane = pieces[0].shape[1] - out_weight.shape[2]
    coming = bring(zip((tokens, mask, embed), held), sems)
    count = len(pieces) // 2
    later = []
    for half in range(2):
        mine_of = pieces[half * count : (half + 1) * count]
        later += bring_in_order(shard, place, mine_of, lane, out_weight.at[half], weight_sems.at[half])
    tokens, mask, embed = held
    rows, cols, _ = tokens.shape
    half, width = rows * cols // 2, near.shape[1]
    to_grid = slots(cols, rows, place[0] // (lons // 2), True)
    update = 0.0
    for lane, (kept, weight) in enumerate(((mine, near), (theirs, far))):
        mixed = dot(to_grid[:, :half], kept[:half, :])
        mixed += dot(to_grid[:, half:], back[:, lane * width : (lane + 1) * width])
        update += dot_t(mixed.astype(jnp.bfloat16), weight[...])
    wait(coming)
    out[...] = land_start(tokens[...], mask[...], embed[...]) + update
    wait(later)


def row_kernel(shard, cols, rows, slopes, spread, *refs):
    place = own_place()
    pieces, (out, tokens, weight, sems, token_sem) = refs[:-5], refs[-5:]
    count = len(pieces) // 2
    fetch = lambda half: bring_in_order(
        shard, place, pieces[half * count : (half + 1) * count], 0, weight.at[half], sems.at[half]
    )
    first_copy = bring([(spread, tokens)], token_sem)
    coming = fetch(0)
    wait(first_copy)
    total = tokens.shape[0]
    block = cols * rows
    lon_count = total // block
    circle = lon_count * cols
    turn, part = lon_count // 2, cols // 2
    spot_q, spot_k = iota((total, total), 0), iota((total, total), 1)

    def lon_of(spot):
        device, slot = spot // block, lax.rem(spot, cols)
        side = device // turn
        holder = lax.rem(device + (slot // part) * turn, lon_count)
        return holder * cols + side * part + lax.rem(slot, part)

    row_of = lambda spot: lax.rem(spot, block) // cols
    gap = jnp.abs(lon_of(spot_q) - lon_of(spot_k))
    distance = jnp.minimum(gap, circle - gap).astype(jnp.float32)
    column = lax.rem(spot_q, cols)
    away = (column // part != spot_q // block // turn).astype(jnp.int32)
    home = lax.rem(spot_q // block + away * turn, lon_count) * block
    home = home + row_of(spot_q) * cols + away * part + lax.rem(column, part)
    homeward = (spot_k == home).astype(jnp.bfloat16)
    same = row_of(spot_q) == row_of(spot_k)
    width = weight.shape[2] // 3
    heads = width // HS
    for half in range(2):
        first = lax.rem(place[1] + half, 2) * heads
        wait(coming)
        if half == 0:
            coming = fetch(1)
        projected = dot(tokens[...], weight[half])
        query = unit_heads(projected[:, :width], 1.0 / math.sqrt(HS))
        keyed = unit_heads(projected[:, width : 2 * width])
        valued = projected[:, 2 * width :].astype(jnp.bfloat16)
        for pair in range(width // PAIR):
            lanes = slice(pair * PAIR, (pair + 1) * PAIR)
            bias = jnp.concatenate(
                [
                    jnp.where(same, distance * -slopes[first + 2 * pair + one], NEVER)
                    for one in range(2)
                ],
                axis=0,
            )
            mixed = two_heads(query[:, lanes], keyed[:, lanes], valued[:, lanes], bias)
            start = half * width + pair * PAIR
            out[:, start : start + PAIR] = dot(homeward, mixed).astype(jnp.bfloat16)


def final_kernel(mixed, middle, weight, out, *refs):
    *held, staged, sems = refs
    coming = bring(zip((mixed, weight, middle), held), sems)
    mixed, weight, middle = held
    width = weight.shape[2]
    wait(coming[:2])
    update = dot_t(mixed[:, :width], weight[0]) + dot_t(mixed[:, width:], weight[1])
    wait(coming[2:])
    staged[...] = (middle[...] + update).reshape(out.shape).astype(jnp.bfloat16)
    wait(bring([(staged, out)], sems))


def fast(
    fields,
    land_mask,
    land_embed,
    column_gain,
    row_gain,
    column_slopes,
    row_slopes,
    column_project,
    column_output,
    row_project,
    row_output,
):
    lon_count = lax.axis_size("lon")
    band, cols, width = fields.shape
    tokens = band * cols
    attend = column_slopes.shape[0] // 2 * HS
    shard = column_project.shape[0]
    embed, column_gain, row_gain = (v.reshape(1, width) for v in (land_embed, column_gain, row_gain))
    mask = land_mask.T
    bf16 = lambda *shape: jax.ShapeDtypeStruct(shape, jnp.bfloat16)
    f32 = lambda *shape: jax.ShapeDtypeStruct(shape, jnp.float32)
    vmem = lambda *arrays: [pltpu.VMEM(v.shape, v.dtype) for v in arrays]
    sems = lambda *shape: [pltpu.SemaphoreType.DMA(shape)]
    after = lax.optimization_barrier
    project_shape = bf16(shard * lon_count, 3 * attend)
    output_shape = bf16(shard * lon_count, attend)
    antipode = lambda value: lax.ppermute(
        value, "lon", at(lambda i: (i + lon_count // 2) % lon_count, lon_count)
    )
    two_lines = lambda value: lax.ppermute(value, "lon", at(lambda i: i ^ (2 * PLANE), lon_count))

    given = (fields, mask, row_project, row_output)
    packed = bf16(tokens // 2 + EXTRA, width)
    keep, send, row_weights = call(
        functools.partial(first_kernel, lon_count),
        (packed, packed, bf16(shard, 4 * attend)),
        "loop_tokens",
        given=given,
        scratch=vmem(*given) + sems(4),
        room=60,
    )
    lines = along_lines(column_project, lon_count)
    output_got, row_got = two_lines(column_output), two_lines(row_weights)
    keep_other = swap_bands(keep)
    *lines, send = after((*lines, send))
    far = antipode(send)
    project = jnp.concatenate([column_project, *lines], axis=0)
    output = jnp.concatenate([column_output, output_got], axis=0)
    row_weights = jnp.concatenate([row_weights, row_got], axis=0)
    project, keep_other = after((project, keep_other))
    project = across_plane(project, lon_count)
    output = doubled(output, PLANE, lon_count)
    far_other = swap_bands(far)

    column_normed = lambda own, other, name: call(
        column_norm_kernel, bf16(tokens, width), name, (own, other, embed, column_gain)
    )
    kept_normed = column_normed(keep, keep_other, "column_normed")
    far_normed = column_normed(far, far_other, "far_normed")
    far_normed, project, output = after((far_normed, project, output))
    project = call(
        functools.partial(order_kernel, shard, True), project_shape, "column_project", project
    )
    row_weights, _ = after((row_weights, far))
    output = across_plane(output, lon_count)
    row_weights = doubled(row_weights, PLANE, lon_count)
    mixed_own, mixed_other = call(
        functools.partial(column_kernel, band),
        (bf16(tokens, attend), bf16(tokens, attend)),
        "column_attention",
        (kept_normed, far_normed, project),
        scalars=(column_slopes,),
        scratch=[pltpu.VMEM((2 * tokens, 3 * attend), jnp.bfloat16)],
        cost=2**18,
    )
    theirs = swap_bands(mixed_other)
    output, row_weights, mixed_own = after((output, row_weights, mixed_own))
    output = call(functools.partial(order_kernel, shard, False), output_shape, "column_output", output)
    output_far = swap_bands(output)

    to_home = jnp.concatenate([mixed_own[tokens // 2 :], theirs[tokens // 2 :]], axis=1)
    row_weights, late = relayed_plane(row_weights, lon_count)
    row_normed = call(
        functools.partial(middle_kernel, cols),
        bf16(tokens, width),
        "row_normed",
        (mixed_own, theirs, output, output_far, keep, far, embed, row_gain),
        cost=2**20,
    )
    spread = lax.all_to_all(row_normed, "lon", split_axis=0, concat_axis=0, tiled=True)
    to_home, row_weights = after((to_home, row_weights))
    home = antipode(to_home)
    row_weights = row_weights + late
    row_weights += [swap_bands(piece) for piece in row_weights]

    row_mixed = call(
        functools.partial(row_kernel, shard, cols, band // lon_count),
        bf16(tokens, 2 * attend),
        "row_attention",
        scalars=(row_slopes,),
        given=(spread, *row_weights),
        scratch=vmem(spread.reshape(tokens, width))
        + [pltpu.VMEM((2, *project_shape.shape), jnp.bfloat16)]
        + sems(2, lon_count)
        + sems(1),
        room=60,
    )
    row_mixed, home = after((row_mixed, home))
    back = lax.all_to_all(row_mixed, "lon", split_axis=0, concat_axis=0, tiled=True)
    given = (fields, mask, embed)
    middle, row_out = call(
        functools.partial(home_kernel, shard, lon_count),
        (f32(tokens, width), bf16(2, *output_shape.shape)),
        "middle",
        (mixed_own, theirs, home, output, output_far),
        given=(*row_weights, *given),
        scratch=vmem(*given) + sems(2, lon_count) + sems(3),
        room=56,
    )
    return call(
        final_kernel,
        bf16(band, cols, width),
        "block_output",
        given=(back, middle, row_out),
        scratch=vmem(back, row_out, middle) + [pltpu.VMEM(fields.shape, jnp.bfloat16)] + sems(3),
        room=60,
        space=pltpu.HBM,
    )


def passed_along(value, axis, by):
    length = lax.axis_size(axis)
    return lax.ppermute(value, axis, [(i, (i + by) % length) for i in range(length)])


def layer_norm(values, gain):
    center = values - jnp.mean(values, axis=-1, keepdims=True)
    spread = jnp.mean(center * center, axis=-1, keepdims=True)
    return center * lax.rsqrt(spread + 1e-05) * gain


def unit_rms(vectors):
    return vectors * lax.rsqrt(jnp.mean(vectors * vectors, axis=-1, keepdims=True) + 1e-06)


def head_split(projected):
    query = unit_rms(projected[..., 0, :]).astype(jnp.bfloat16)
    keyed = unit_rms(projected[..., 1, :]).astype(jnp.bfloat16)
    valued = projected[..., 2, :].astype(jnp.bfloat16)
    return (query, keyed, valued)


def gather_bands(normed):
    return lax.all_gather(normed, "lat", axis=0, tiled=True)


def sum_heads(partial_value):
    return lax.psum_scatter(
        partial_value.astype(jnp.bfloat16), "lat", scatter_dimension=0, tiled=True
    ).astype(jnp.float32)


def project_in(normed, weight):
    return jnp.dot(
        normed,
        lax.all_gather(weight, "lon", axis=0, tiled=True),
        preferred_element_type=jnp.float32,
    )


def project_out(mixed, weight):
    return lax.dot_general(
        mixed,
        lax.all_gather(weight, "lon", axis=0, tiled=True),
        (((1,), (1,)), ((), ())),
        preferred_element_type=jnp.float32,
    )


def column_attend(query, column_kv, far_kv, slopes):
    total_rows = column_kv.shape[0]
    keyed = jnp.concatenate([column_kv[..., :HS], far_kv[..., :HS]], axis=0)
    valued = jnp.concatenate([column_kv[..., HS:], far_kv[..., HS:]], axis=0)
    scores = jnp.einsum("rchd,schd->chrs", query, keyed, preferred_element_type=jnp.float32)
    rows_here = jnp.arange(query.shape[0], dtype=jnp.int32)
    key_rows = jnp.arange(total_rows, dtype=jnp.int32)
    near_dist = jnp.abs(rows_here[:, None] - key_rows[None, :])
    pair_sum = rows_here[:, None] + key_rows[None, :]
    far_dist = jnp.minimum(pair_sum + 1, 2 * total_rows - 1 - pair_sum)
    distance = jnp.concatenate([near_dist, far_dist], axis=1).astype(jnp.float32)
    weight = jnp.exp(scores * (1.0 / math.sqrt(HS)) - slopes[None, :, None, None] * distance)
    prob = (weight / jnp.sum(weight, axis=-1, keepdims=True)).astype(jnp.bfloat16)
    mixed = jnp.einsum("chrs,schd->rchd", prob, valued, preferred_element_type=jnp.float32)
    return mixed.astype(jnp.bfloat16).reshape(query.shape[0], query.shape[1], -1)


def general(
    fields,
    land_mask,
    land_embed,
    column_gain,
    row_gain,
    column_slopes,
    row_slopes,
    column_project,
    column_output,
    row_project,
    row_output,
):
    lon_count = lax.axis_size("lon")
    lat_count = lax.axis_size("lat")
    band_rows, local_cols, width = fields.shape
    lat_place = lax.axis_index("lat")
    head_total = column_slopes.shape[0]
    head_share = head_total // lat_count
    first_head = lat_place * head_share
    start = fields.astype(jnp.float32) + land_mask.astype(jnp.float32)[..., None] * land_embed
    normed = layer_norm(start, column_gain).astype(jnp.bfloat16)
    whole = gather_bands(normed)
    projected = project_in(whole.reshape(-1, width), column_project)
    query, keyed, valued = head_split(
        projected.reshape(band_rows * lat_count, local_cols, head_share, 3, HS)
    )
    column_kv = jnp.concatenate([keyed, valued], axis=-1).reshape(
        band_rows * lat_count, local_cols, -1
    )
    slopes = lax.dynamic_slice_in_dim(column_slopes, first_head, head_share)
    far_kv = passed_along(column_kv, "lon", lon_count // 2)
    shaped = column_kv.shape[:2] + (head_share, 2 * HS)
    mixed = column_attend(query, column_kv.reshape(shaped), far_kv.reshape(shaped), slopes)
    partial_value = project_out(mixed.reshape(-1, head_share * HS), column_output)
    update = sum_heads(partial_value.reshape(band_rows * lat_count, local_cols, width))
    middle = start + update
    total_rows = band_rows * lat_count
    row_normed = layer_norm(middle, row_gain).astype(jnp.bfloat16)
    whole_rows = gather_bands(row_normed)
    projected = project_in(whole_rows.reshape(-1, width), row_project)
    query, keyed, valued = head_split(projected.reshape(total_rows, local_cols, head_share, 3, HS))
    packed = jnp.stack([query, keyed, valued], axis=3)
    parts = lax.all_to_all(packed, "lon", split_axis=0, concat_axis=1, tiled=True)
    few_rows, all_cols = (parts.shape[0], parts.shape[1])
    scores = jnp.einsum(
        "rchd,rehd->rhce", parts[..., 0, :], parts[..., 1, :], preferred_element_type=jnp.float32
    )
    cols_here = jnp.arange(all_cols, dtype=jnp.int32)
    gap = jnp.abs(cols_here[:, None] - cols_here[None, :])
    cycle_dist = jnp.minimum(gap, all_cols - gap).astype(jnp.float32)
    row_slope = lax.dynamic_slice_in_dim(row_slopes, first_head, head_share)
    weight = jnp.exp(scores * (1.0 / math.sqrt(HS)) - row_slope[None, :, None, None] * cycle_dist)
    prob = (weight / jnp.sum(weight, axis=-1, keepdims=True)).astype(jnp.bfloat16)
    row_mixed = jnp.einsum(
        "rhce,rehd->rchd", prob, parts[..., 2, :], preferred_element_type=jnp.float32
    )
    row_mixed = row_mixed.astype(jnp.bfloat16)
    back = lax.all_to_all(row_mixed, "lon", split_axis=1, concat_axis=0, tiled=True)
    partial_value = project_out(back.reshape(-1, head_share * HS), row_output)
    final_update = sum_heads(partial_value.reshape(total_rows, local_cols, width))
    return (middle + final_update).astype(jnp.bfloat16)


def solution(mesh):
    in_specs = (
        P("lat", "lon", None),
        P("lat", "lon"),
        P(),
        P(),
        P(),
        P(),
        P(),
        P("lon", "lat"),
        P("lon", "lat"),
        P("lon", "lat"),
        P("lon", "lat"),
    )
    out_specs = P(("ens", "lat"), "lon", None)

    def shards(fields, *rest):
        length = lax.axis_size("lon")
        suits = fields.shape[0] % length == 0 and length == 4 * PLANE
        return (fast if suits else general)(fields, *rest)

    return jax.shard_map(shards, mesh=mesh, in_specs=in_specs, out_specs=out_specs, check_vma=False)
```

```python
import functools
import math

import jax
import jax.numpy as jnp
from jax import lax
from jax.experimental import pallas as pl
from jax.experimental.pallas import tpu as pltpu
from jax.sharding import PartitionSpec as P

HS = 64
PAIR = 2 * HS
PLANE = 4
NEVER = -1e30
EXTRA = 16


def at(place, length):
    return [(i, place(i)) for i in range(length)]


def swap_bands(value):
    return lax.ppermute(value, "lat", at(lambda i: 1 - i, 2))


SCALARS = pl.BlockSpec(memory_space=pltpu.SMEM)


def call(
    kernel,
    out,
    name,
    arrays=(),
    scalars=(),
    given=(),
    scratch=(),
    cost=2**10,
    room=24,
    space=pltpu.VMEM,
    given_space=pltpu.HBM,
):
    return pl.pallas_call(
        kernel,
        out_shape=out,
        in_specs=[SCALARS] * len(scalars)
        + [pl.BlockSpec(memory_space=pltpu.VMEM)] * len(arrays)
        + [pl.BlockSpec(memory_space=given_space)] * len(given),
        out_specs=jax.tree.map(lambda _: pl.BlockSpec(memory_space=space), out),
        scratch_shapes=scratch,
        compiler_params=pltpu.CompilerParams(vmem_limit_bytes=room * 2**20),
        cost_estimate=pl.CostEstimate(flops=2**10, bytes_accessed=cost, transcendentals=0),
        name=name,
    )(*scalars, *arrays, *given)


def own_place():
    return lax.axis_index("lon"), lax.axis_index("lat")


def dot(a, b):
    return jnp.dot(a, b, preferred_element_type=jnp.float32)


def dot_t(a, b):
    return lax.dot_general(a, b, (((1,), (1,)), ((), ())), preferred_element_type=jnp.float32)


def iota(shape, axis):
    return lax.broadcasted_iota(jnp.int32, shape, axis)


def bring(pairs, sems):
    copies = [pltpu.make_async_copy(ref, held, sems.at[i]) for i, (ref, held) in enumerate(pairs)]
    for copy in copies:
        copy.start()
    return copies


def wait(copies):
    for copy in copies:
        copy.wait()


def along_lines(weight, length):
    steps = range(PLANE, length, PLANE)
    return [lax.ppermute(weight, "lon", at(lambda i: i ^ k, length)) for k in steps]


def doubled(weight, step, length):
    got = lax.ppermute(weight, "lon", at(lambda i: i ^ step, length))
    half = weight.shape[0] // 2
    return jnp.concatenate([weight[:half], got[:half], weight[half:], got[half:]], axis=0)


def across_plane(part, length):
    return [part] + [lax.ppermute(part, "lon", at(lambda i: i ^ k, length)) for k in range(1, PLANE)]


def relayed_plane(part, length):
    half = part.shape[0] // 2
    step = lambda value, k: lax.ppermute(value, "lon", at(lambda i: i ^ k, length))
    first, second = step(part, 1), step(part, 2)
    return [part, first, second], [step(second[:half], 1), step(first[half:], 2)]


def by_kind(weight):
    heads = weight.shape[1] // (3 * HS)
    block = lambda kind, head: weight[:, (3 * head + kind) * HS : (3 * head + kind + 1) * HS]
    return jnp.concatenate([block(kind, head) for kind in range(3) for head in range(heads)], axis=1)


def places(shard, place, pieces):
    line, spot = place[0] // PLANE, place[0] % PLANE
    lines = pieces[0].shape[0] // shard
    blocks = [(piece, k) for piece in pieces for k in range(piece.shape[0] // shard)]
    for number, (piece, k) in enumerate(blocks):
        owner = lax.bitwise_xor(line, number % lines) * PLANE
        owner += lax.bitwise_xor(spot, number // lines)
        there = pl.ds(pl.multiple_of(owner * shard, shard), shard)
        yield piece, slice(k * shard, (k + 1) * shard), there


def order_kernel(shard, sort, w0, w1, w2, w3, out):
    place = own_place()
    for piece, here, there in places(shard, place, (w0, w1, w2, w3)):
        out[there, :] = by_kind(piece[here, :]) if sort else piece[here, :]


def bring_in_order(shard, place, pieces, lane, target, sems):
    lanes = slice(lane, lane + target.shape[1])
    return bring(
        [
            (piece.at[here, lanes], target.at[there, :])
            for piece, here, there in places(shard, place, pieces)
        ],
        sems,
    )


def norm(values, gain):
    center = values - jnp.mean(values, axis=-1, keepdims=True)
    spread = jnp.mean(center * center, axis=-1, keepdims=True)
    return center * lax.rsqrt(spread + 1e-05) * gain


def land_start(tokens, mask, embed):
    cols, rows = mask.shape
    total = rows * cols
    row_of = (iota((total, rows), 0) // cols == iota((total, rows), 1)).astype(jnp.bfloat16)
    spread = dot_t(row_of, mask.astype(jnp.bfloat16))
    own = iota((total, cols), 0) % cols == iota((total, cols), 1)
    land = jnp.sum(jnp.where(own, spread, 0.0), axis=1, keepdims=True)
    return tokens.astype(jnp.float32).reshape(total, tokens.shape[2]) + land * embed


def packed_start(packed, embed):
    total = packed.shape[0] - EXTRA
    row = packed[total : total + 1, :total].astype(jnp.float32)
    same = iota((total, total), 0) == iota((total, total), 1)
    land = jnp.sum(jnp.where(same, row, 0.0), axis=1, keepdims=True)
    return packed[:total, :].astype(jnp.float32) + land * embed


def slots(cols, rows, side, inverse=False):
    total = cols * rows
    spot, grid = iota((total, total), int(inverse)), iota((total, total), int(not inverse))
    column = lax.rem(spot // rows + side * (cols // 2), cols)
    return (grid == lax.rem(spot, rows) * cols + column).astype(jnp.bfloat16)


def first_kernel(lons, tokens, mask, project, output, keep, send, packed, *scratch):
    place = own_place()
    *held, sems = scratch
    coming = bring(zip((tokens, mask, project, output), held), sems)
    tokens, mask, project, output = held
    rows, cols, width = tokens.shape
    half = rows * cols // 2
    side = place[0] // (lons // 2)
    to_slots = slots(cols, rows, side)
    wait(coming[:2])
    flat = tokens[...].astype(jnp.float32).reshape(rows * cols, width).astype(jnp.bfloat16)
    in_slots = dot(to_slots, flat).astype(jnp.bfloat16)
    land = mask[...].astype(jnp.float32)
    parts = [land[c : c + 1, :] for c in range(cols)]
    halves = [jnp.concatenate(parts[: cols // 2], axis=1), jnp.concatenate(parts[cols // 2 :], axis=1)]
    for k, out in enumerate((keep, send)):
        out[:half, :] = in_slots[k * half : (k + 1) * half]
        out[half:, :] = jnp.zeros((EXTRA, width), jnp.bfloat16)
        row = jnp.where(side == k, halves[0], halves[1])
        out[half:, :half] = jnp.broadcast_to(row, (EXTRA, half)).astype(jnp.bfloat16)
    wait(coming[2:])
    split = project.shape[1]
    packed[:, :split] = by_kind(project[...])
    packed[:, split:] = output[...]


def column_norm_kernel(own, other, embed, gain, out):
    half = own.shape[0] - EXTRA
    for k, ref in enumerate((own, other)):
        normed = norm(packed_start(ref[...], embed[...]), gain[...])
        out[k * half : (k + 1) * half, :] = normed.astype(jnp.bfloat16)


def unit_heads(vectors, scale=1.0):
    width = vectors.shape[1]
    same = (iota((width, width), 0) // HS == iota((width, width), 1) // HS).astype(jnp.bfloat16)
    total = dot((vectors * vectors).astype(jnp.bfloat16), same)
    return (vectors * (lax.rsqrt(total * (1.0 / HS) + 1e-06) * scale)).astype(jnp.bfloat16)


def two_heads(query, keyed, valued, bias):
    rows = query.shape[0]
    first = iota(query.shape, 1) < HS
    zero = jnp.zeros_like(query)
    stacked = jnp.concatenate([jnp.where(first, query, zero), jnp.where(first, zero, query)], axis=0)
    weight = jnp.exp(dot_t(stacked, keyed) + bias).astype(jnp.bfloat16)
    widened = jnp.concatenate([valued, jnp.ones_like(valued)], axis=1)
    mixed = dot(weight, widened)
    mixed = mixed[:, :PAIR] / mixed[:, PAIR:]
    return jnp.where(first, mixed[:rows], mixed[rows:]).astype(jnp.bfloat16)


def column_kernel(band, slopes, tokens, far_tokens, weight, out_own, out_other, qkv):
    place = own_place()
    block = tokens.shape[0] // 2
    loops = block // band
    width = weight.shape[1] // 3
    for half, ref in enumerate((tokens, far_tokens)):
        projected = dot(ref[...], weight[...])
        at_rows = slice(half * 2 * block, (half + 1) * 2 * block)
        qkv[at_rows, :width] = unit_heads(projected[:, :width], 1.0 / math.sqrt(HS))
        qkv[at_rows, width : 2 * width] = unit_heads(projected[:, width : 2 * width])
        qkv[at_rows, 2 * width :] = projected[:, 2 * width :].astype(jnp.bfloat16)
    total = 2 * band
    shape = (2 * total, 2 * total)
    spot_q, spot_k = iota(shape, 0), iota(shape, 1)
    shift = place[1] * band
    row_q, row_k = lax.rem(spot_q + shift, total), lax.rem(spot_k + shift, total)
    pair_sum = row_q + row_k
    beyond = jnp.minimum(pair_sum + 1, 2 * total - 1 - pair_sum)
    here = (spot_q < total) == (spot_k < total)
    distance = jnp.where(here, jnp.abs(row_q - row_k), beyond).astype(jnp.float32)
    first = place[1] * (width // HS)
    for pair in range(width // PAIR):
        bias = jnp.concatenate(
            [distance * -slopes[first + 2 * pair + one] for one in range(2)], axis=0
        )
        lanes = slice(pair * PAIR, (pair + 1) * PAIR)
        for loop in range(loops):
            starts = [part * block + loop * band for part in range(4)]
            query, keyed, valued = (
                jnp.concatenate(
                    [
                        qkv[at : at + band, kind * width + lanes.start : kind * width + lanes.stop]
                        for at in starts
                    ],
                    axis=0,
                )
                for kind in range(3)
            )
            mixed = two_heads(query, keyed, valued, bias)
            for part in range(4):
                out = (out_own, out_other)[part % 2]
                slot = (part // 2) * loops + loop
                out[slot * band : (slot + 1) * band, lanes] = mixed[part * band : (part + 1) * band]


def middle_kernel(cols, mine, theirs, near, far, kept, got, embed, gain, out):
    update = dot_t(mine[...], near[...]) + dot_t(theirs[...], far[...])
    parts = [packed_start(ref[...], embed[...]) for ref in (kept, got)]
    middle = jnp.concatenate(parts, axis=0) + update
    normed = norm(middle, gain[...]).astype(jnp.bfloat16)
    by_row = slots(cols, normed.shape[0] // cols, 0, True)
    out[...] = dot(by_row, normed).astype(jnp.bfloat16)


def home_kernel(shard, lons, mine, theirs, back, near, far, *refs):
    place = own_place()
    pieces, (tokens, mask, embed, out, out_weight, *held, weight_sems, sems) = refs[:-10], refs[-10:]
    lane = pieces[0].shape[1] - out_weight.shape[2]
    coming = bring(zip((tokens, mask, embed), held), sems)
    count = len(pieces) // 2
    later = []
    for half in range(2):
        mine_of = pieces[half * count : (half + 1) * count]
        later += bring_in_order(shard, place, mine_of, lane, out_weight.at[half], weight_sems.at[half])
    tokens, mask, embed = held
    rows, cols, _ = tokens.shape
    half, width = rows * cols // 2, near.shape[1]
    to_grid = slots(cols, rows, place[0] // (lons // 2), True)
    update = 0.0
    for lane, (kept, weight) in enumerate(((mine, near), (theirs, far))):
        mixed = dot(to_grid[:, :half], kept[:half, :])
        mixed += dot(to_grid[:, half:], back[:, lane * width : (lane + 1) * width])
        update += dot_t(mixed.astype(jnp.bfloat16), weight[...])
    wait(coming)
    out[...] = land_start(tokens[...], mask[...], embed[...]) + update
    wait(later)


def row_kernel(shard, cols, rows, slopes, spread, *refs):
    place = own_place()
    pieces, (out, tokens, weight, sems, token_sem) = refs[:-5], refs[-5:]
    count = len(pieces) // 2
    fetch = lambda half: bring_in_order(
        shard, place, pieces[half * count : (half + 1) * count], 0, weight.at[half], sems.at[half]
    )
    first_copy = bring([(spread, tokens)], token_sem)
    coming = fetch(0)
    total = tokens.shape[0]
    block = cols * rows
    lon_count = total // block
    circle = lon_count * cols
    turn, part = lon_count // 2, cols // 2
    spot_q, spot_k = iota((total, total), 0), iota((total, total), 1)

    def lon_of(spot):
        device, slot = spot // block, lax.rem(spot, cols)
        side = device // turn
        holder = lax.rem(device + (slot // part) * turn, lon_count)
        return holder * cols + side * part + lax.rem(slot, part)

    row_of = lambda spot: lax.rem(spot, block) // cols
    gap = jnp.abs(lon_of(spot_q) - lon_of(spot_k))
    distance = jnp.minimum(gap, circle - gap).astype(jnp.float32)
    column = lax.rem(spot_q, cols)
    away = (column // part != spot_q // block // turn).astype(jnp.int32)
    home = lax.rem(spot_q // block + away * turn, lon_count) * block
    home = home + row_of(spot_q) * cols + away * part + lax.rem(column, part)
    homeward = (spot_k == home).astype(jnp.bfloat16)
    same = row_of(spot_q) == row_of(spot_k)
    width = weight.shape[2] // 3
    heads = width // HS
    wait(first_copy)
    for half in range(2):
        first = lax.rem(place[1] + half, 2) * heads
        wait(coming)
        if half == 0:
            coming = fetch(1)
        projected = dot(tokens[...], weight[half])
        query = unit_heads(projected[:, :width], 1.0 / math.sqrt(HS))
        keyed = unit_heads(projected[:, width : 2 * width])
        valued = projected[:, 2 * width :].astype(jnp.bfloat16)
        mixed = []
        for pair in range(width // PAIR):
            lanes = slice(pair * PAIR, (pair + 1) * PAIR)
            bias = jnp.concatenate(
                [
                    jnp.where(same, distance * -slopes[first + 2 * pair + one], NEVER)
                    for one in range(2)
                ],
                axis=0,
            )
            mixed.append(two_heads(query[:, lanes], keyed[:, lanes], valued[:, lanes], bias))
        mixed = jnp.concatenate(mixed, axis=1)
        out[:, half * width : (half + 1) * width] = dot(homeward, mixed).astype(jnp.bfloat16)


def final_kernel(mixed, middle, weight, out, *refs):
    *held, staged, sems = refs
    coming = bring(zip((mixed, weight, middle), held), sems)
    mixed, weight, middle = held
    width = weight.shape[2]
    wait(coming[:2])
    update = dot_t(mixed[:, :width], weight[0]) + dot_t(mixed[:, width:], weight[1])
    wait(coming[2:])
    staged[...] = (middle[...] + update).reshape(out.shape).astype(jnp.bfloat16)
    wait(bring([(staged, out)], sems))


def fast(
    fields,
    land_mask,
    land_embed,
    column_gain,
    row_gain,
    column_slopes,
    row_slopes,
    column_project,
    column_output,
    row_project,
    row_output,
):
    lon_count = lax.axis_size("lon")
    band, cols, width = fields.shape
    tokens = band * cols
    attend = column_slopes.shape[0] // 2 * HS
    shard = column_project.shape[0]
    embed, column_gain, row_gain = (v.reshape(1, width) for v in (land_embed, column_gain, row_gain))
    mask = land_mask.T
    bf16 = lambda *shape: jax.ShapeDtypeStruct(shape, jnp.bfloat16)
    f32 = lambda *shape: jax.ShapeDtypeStruct(shape, jnp.float32)
    vmem = lambda *arrays: [pltpu.VMEM(v.shape, v.dtype) for v in arrays]
    sems = lambda *shape: [pltpu.SemaphoreType.DMA(shape)]
    after = lax.optimization_barrier
    project_shape = bf16(shard * lon_count, 3 * attend)
    output_shape = bf16(shard * lon_count, attend)
    antipode = lambda value: lax.ppermute(
        value, "lon", at(lambda i: (i + lon_count // 2) % lon_count, lon_count)
    )
    two_lines = lambda value: lax.ppermute(value, "lon", at(lambda i: i ^ (2 * PLANE), lon_count))

    given = (fields, mask, row_project, row_output)
    packed = bf16(tokens // 2 + EXTRA, width)
    keep, send, row_weights = call(
        functools.partial(first_kernel, lon_count),
        (packed, packed, bf16(shard, 4 * attend)),
        "loop_tokens",
        given=given,
        scratch=vmem(*given) + sems(4),
        room=60,
    )
    lines = along_lines(column_project, lon_count)
    output_got, row_got = two_lines(column_output), two_lines(row_weights)
    keep_other = swap_bands(keep)
    *lines, send = after((*lines, send))
    far = antipode(send)
    project = jnp.concatenate([column_project, *lines], axis=0)
    output = jnp.concatenate([column_output, output_got], axis=0)
    row_weights = jnp.concatenate([row_weights, row_got], axis=0)
    project, keep_other = after((project, keep_other))
    project = across_plane(project, lon_count)
    output = doubled(output, PLANE, lon_count)
    far_other = swap_bands(far)

    column_normed = lambda own, other, name: call(
        column_norm_kernel, bf16(tokens, width), name, (own, other, embed, column_gain)
    )
    kept_normed = column_normed(keep, keep_other, "column_normed")
    far_normed = column_normed(far, far_other, "far_normed")
    far_normed, project, output = after((far_normed, project, output))
    project = call(
        functools.partial(order_kernel, shard, True), project_shape, "column_project", project
    )
    row_weights, _ = after((row_weights, far))
    output = across_plane(output, lon_count)
    row_weights = doubled(row_weights, PLANE, lon_count)
    mixed_own, mixed_other = call(
        functools.partial(column_kernel, band),
        (bf16(tokens, attend), bf16(tokens, attend)),
        "column_attention",
        (kept_normed, far_normed, project),
        scalars=(column_slopes,),
        scratch=[pltpu.VMEM((2 * tokens, 3 * attend), jnp.bfloat16)],
        cost=2**18,
    )
    theirs = swap_bands(mixed_other)
    output, row_weights, mixed_own = after((output, row_weights, mixed_own))
    output = call(functools.partial(order_kernel, shard, False), output_shape, "column_output", output)
    output_far = swap_bands(output)

    to_home = jnp.concatenate([mixed_own[tokens // 2 :], theirs[tokens // 2 :]], axis=1)
    row_weights, late = relayed_plane(row_weights, lon_count)
    row_normed = call(
        functools.partial(middle_kernel, cols),
        bf16(tokens, width),
        "row_normed",
        (mixed_own, theirs, output, output_far, keep, far, embed, row_gain),
        cost=2**20,
    )
    spread = lax.all_to_all(row_normed, "lon", split_axis=0, concat_axis=0, tiled=True)
    to_home, row_weights = after((to_home, row_weights))
    home = antipode(to_home)
    row_weights = row_weights + late
    row_weights += [swap_bands(piece) for piece in row_weights]

    row_mixed = call(
        functools.partial(row_kernel, shard, cols, band // lon_count),
        bf16(tokens, 2 * attend),
        "row_attention",
        scalars=(row_slopes,),
        given=(spread, *row_weights),
        scratch=vmem(spread.reshape(tokens, width))
        + [pltpu.VMEM((2, *project_shape.shape), jnp.bfloat16)]
        + sems(2, lon_count)
        + sems(1),
        room=51,
        given_space=pl.ANY,
    )
    row_mixed, home = after((row_mixed, home))
    back = lax.all_to_all(row_mixed, "lon", split_axis=0, concat_axis=0, tiled=True)
    given = (fields, mask, embed)
    middle, row_out = call(
        functools.partial(home_kernel, shard, lon_count),
        (f32(tokens, width), bf16(2, *output_shape.shape)),
        "middle",
        (mixed_own, theirs, home, output, output_far),
        given=(*row_weights, *given),
        scratch=vmem(*given) + sems(2, lon_count) + sems(3),
        room=56,
    )
    return call(
        final_kernel,
        bf16(band, cols, width),
        "block_output",
        given=(back, middle, row_out),
        scratch=vmem(back, row_out, middle) + [pltpu.VMEM(fields.shape, jnp.bfloat16)] + sems(3),
        room=60,
        space=pltpu.HBM,
    )


def passed_along(value, axis, by):
    length = lax.axis_size(axis)
    return lax.ppermute(value, axis, [(i, (i + by) % length) for i in range(length)])


def layer_norm(values, gain):
    center = values - jnp.mean(values, axis=-1, keepdims=True)
    spread = jnp.mean(center * center, axis=-1, keepdims=True)
    return center * lax.rsqrt(spread + 1e-05) * gain


def unit_rms(vectors):
    return vectors * lax.rsqrt(jnp.mean(vectors * vectors, axis=-1, keepdims=True) + 1e-06)


def head_split(projected):
    query = unit_rms(projected[..., 0, :]).astype(jnp.bfloat16)
    keyed = unit_rms(projected[..., 1, :]).astype(jnp.bfloat16)
    valued = projected[..., 2, :].astype(jnp.bfloat16)
    return (query, keyed, valued)


def gather_bands(normed):
    return lax.all_gather(normed, "lat", axis=0, tiled=True)


def sum_heads(partial_value):
    return lax.psum_scatter(
        partial_value.astype(jnp.bfloat16), "lat", scatter_dimension=0, tiled=True
    ).astype(jnp.float32)


def project_in(normed, weight):
    return jnp.dot(
        normed,
        lax.all_gather(weight, "lon", axis=0, tiled=True),
        preferred_element_type=jnp.float32,
    )


def project_out(mixed, weight):
    return lax.dot_general(
        mixed,
        lax.all_gather(weight, "lon", axis=0, tiled=True),
        (((1,), (1,)), ((), ())),
        preferred_element_type=jnp.float32,
    )


def column_attend(query, column_kv, far_kv, slopes):
    total_rows = column_kv.shape[0]
    keyed = jnp.concatenate([column_kv[..., :HS], far_kv[..., :HS]], axis=0)
    valued = jnp.concatenate([column_kv[..., HS:], far_kv[..., HS:]], axis=0)
    scores = jnp.einsum("rchd,schd->chrs", query, keyed, preferred_element_type=jnp.float32)
    rows_here = jnp.arange(query.shape[0], dtype=jnp.int32)
    key_rows = jnp.arange(total_rows, dtype=jnp.int32)
    near_dist = jnp.abs(rows_here[:, None] - key_rows[None, :])
    pair_sum = rows_here[:, None] + key_rows[None, :]
    far_dist = jnp.minimum(pair_sum + 1, 2 * total_rows - 1 - pair_sum)
    distance = jnp.concatenate([near_dist, far_dist], axis=1).astype(jnp.float32)
    weight = jnp.exp(scores * (1.0 / math.sqrt(HS)) - slopes[None, :, None, None] * distance)
    prob = (weight / jnp.sum(weight, axis=-1, keepdims=True)).astype(jnp.bfloat16)
    mixed = jnp.einsum("chrs,schd->rchd", prob, valued, preferred_element_type=jnp.float32)
    return mixed.astype(jnp.bfloat16).reshape(query.shape[0], query.shape[1], -1)


def general(
    fields,
    land_mask,
    land_embed,
    column_gain,
    row_gain,
    column_slopes,
    row_slopes,
    column_project,
    column_output,
    row_project,
    row_output,
):
    lon_count = lax.axis_size("lon")
    lat_count = lax.axis_size("lat")
    band_rows, local_cols, width = fields.shape
    lat_place = lax.axis_index("lat")
    head_total = column_slopes.shape[0]
    head_share = head_total // lat_count
    first_head = lat_place * head_share
    start = fields.astype(jnp.float32) + land_mask.astype(jnp.float32)[..., None] * land_embed
    normed = layer_norm(start, column_gain).astype(jnp.bfloat16)
    whole = gather_bands(normed)
    projected = project_in(whole.reshape(-1, width), column_project)
    query, keyed, valued = head_split(
        projected.reshape(band_rows * lat_count, local_cols, head_share, 3, HS)
    )
    column_kv = jnp.concatenate([keyed, valued], axis=-1).reshape(
        band_rows * lat_count, local_cols, -1
    )
    slopes = lax.dynamic_slice_in_dim(column_slopes, first_head, head_share)
    far_kv = passed_along(column_kv, "lon", lon_count // 2)
    shaped = column_kv.shape[:2] + (head_share, 2 * HS)
    mixed = column_attend(query, column_kv.reshape(shaped), far_kv.reshape(shaped), slopes)
    partial_value = project_out(mixed.reshape(-1, head_share * HS), column_output)
    update = sum_heads(partial_value.reshape(band_rows * lat_count, local_cols, width))
    middle = start + update
    total_rows = band_rows * lat_count
    row_normed = layer_norm(middle, row_gain).astype(jnp.bfloat16)
    whole_rows = gather_bands(row_normed)
    projected = project_in(whole_rows.reshape(-1, width), row_project)
    query, keyed, valued = head_split(projected.reshape(total_rows, local_cols, head_share, 3, HS))
    packed = jnp.stack([query, keyed, valued], axis=3)
    parts = lax.all_to_all(packed, "lon", split_axis=0, concat_axis=1, tiled=True)
    few_rows, all_cols = (parts.shape[0], parts.shape[1])
    scores = jnp.einsum(
        "rchd,rehd->rhce", parts[..., 0, :], parts[..., 1, :], preferred_element_type=jnp.float32
    )
    cols_here = jnp.arange(all_cols, dtype=jnp.int32)
    gap = jnp.abs(cols_here[:, None] - cols_here[None, :])
    cycle_dist = jnp.minimum(gap, all_cols - gap).astype(jnp.float32)
    row_slope = lax.dynamic_slice_in_dim(row_slopes, first_head, head_share)
    weight = jnp.exp(scores * (1.0 / math.sqrt(HS)) - row_slope[None, :, None, None] * cycle_dist)
    prob = (weight / jnp.sum(weight, axis=-1, keepdims=True)).astype(jnp.bfloat16)
    row_mixed = jnp.einsum(
        "rhce,rehd->rchd", prob, parts[..., 2, :], preferred_element_type=jnp.float32
    )
    row_mixed = row_mixed.astype(jnp.bfloat16)
    back = lax.all_to_all(row_mixed, "lon", split_axis=1, concat_axis=0, tiled=True)
    partial_value = project_out(back.reshape(-1, head_share * HS), row_output)
    final_update = sum_heads(partial_value.reshape(total_rows, local_cols, width))
    return (middle + final_update).astype(jnp.bfloat16)


def solution(mesh):
    in_specs = (
        P("lat", "lon", None),
        P("lat", "lon"),
        P(),
        P(),
        P(),
        P(),
        P(),
        P("lon", "lat"),
        P("lon", "lat"),
        P("lon", "lat"),
        P("lon", "lat"),
    )
    out_specs = P(("ens", "lat"), "lon", None)

    def shards(fields, *rest):
        length = lax.axis_size("lon")
        suits = fields.shape[0] % length == 0 and length == 4 * PLANE
        return (fast if suits else general)(fields, *rest)

    return jax.shard_map(shards, mesh=mesh, in_specs=in_specs, out_specs=out_specs, check_vma=False)
```

```python
import functools
import math

import jax
import jax.numpy as jnp
from jax import lax
from jax.experimental import pallas as pl
from jax.experimental.pallas import tpu as pltpu
from jax.sharding import PartitionSpec as P

HS = 64
PAIR = 2 * HS
PLANE = 4
NEVER = -1e30
EXTRA = 16


def at(place, length):
    return [(i, place(i)) for i in range(length)]


def swap_bands(value):
    return lax.ppermute(value, "lat", at(lambda i: 1 - i, 2))


SCALARS = pl.BlockSpec(memory_space=pltpu.SMEM)


def call(
    kernel,
    out,
    name,
    arrays=(),
    scalars=(),
    given=(),
    scratch=(),
    cost=2**10,
    room=24,
    space=pltpu.VMEM,
    given_space=pltpu.HBM,
):
    return pl.pallas_call(
        kernel,
        out_shape=out,
        in_specs=[SCALARS] * len(scalars)
        + [pl.BlockSpec(memory_space=pltpu.VMEM)] * len(arrays)
        + [pl.BlockSpec(memory_space=given_space)] * len(given),
        out_specs=jax.tree.map(lambda _: pl.BlockSpec(memory_space=space), out),
        scratch_shapes=scratch,
        compiler_params=pltpu.CompilerParams(vmem_limit_bytes=room * 2**20),
        cost_estimate=pl.CostEstimate(flops=2**10, bytes_accessed=cost, transcendentals=0),
        name=name,
    )(*scalars, *arrays, *given)


def own_place():
    return lax.axis_index("lon"), lax.axis_index("lat")


def dot(a, b):
    return jnp.dot(a, b, preferred_element_type=jnp.float32)


def dot_t(a, b):
    return lax.dot_general(a, b, (((1,), (1,)), ((), ())), preferred_element_type=jnp.float32)


def iota(shape, axis):
    return lax.broadcasted_iota(jnp.int32, shape, axis)


def bring(pairs, sems):
    copies = [pltpu.make_async_copy(ref, held, sems.at[i]) for i, (ref, held) in enumerate(pairs)]
    for copy in copies:
        copy.start()
    return copies


def wait(copies):
    for copy in copies:
        copy.wait()


def along_lines(weight, length):
    steps = range(PLANE, length, PLANE)
    return [lax.ppermute(weight, "lon", at(lambda i: i ^ k, length)) for k in steps]


def doubled(weight, step, length):
    got = lax.ppermute(weight, "lon", at(lambda i: i ^ step, length))
    half = weight.shape[0] // 2
    return jnp.concatenate([weight[:half], got[:half], weight[half:], got[half:]], axis=0)


def across_plane(part, length):
    return [part] + [lax.ppermute(part, "lon", at(lambda i: i ^ k, length)) for k in range(1, PLANE)]


def relayed_plane(part, length):
    half = part.shape[0] // 2
    step = lambda value, k: lax.ppermute(value, "lon", at(lambda i: i ^ k, length))
    first, second = step(part, 1), step(part, 2)
    return [part, first, second], [step(second[:half], 1), step(first[half:], 2)]


def by_kind(weight):
    heads = weight.shape[1] // (3 * HS)
    block = lambda kind, head: weight[:, (3 * head + kind) * HS : (3 * head + kind + 1) * HS]
    return jnp.concatenate([block(kind, head) for kind in range(3) for head in range(heads)], axis=1)


def places(shard, place, pieces):
    line, spot = place[0] // PLANE, place[0] % PLANE
    lines = pieces[0].shape[0] // shard
    blocks = [(piece, k) for piece in pieces for k in range(piece.shape[0] // shard)]
    for number, (piece, k) in enumerate(blocks):
        owner = lax.bitwise_xor(line, number % lines) * PLANE
        owner += lax.bitwise_xor(spot, number // lines)
        there = pl.ds(pl.multiple_of(owner * shard, shard), shard)
        yield piece, slice(k * shard, (k + 1) * shard), there


def order_kernel(shard, sort, w0, w1, w2, w3, out):
    place = own_place()
    for piece, here, there in places(shard, place, (w0, w1, w2, w3)):
        out[there, :] = by_kind(piece[here, :]) if sort else piece[here, :]


def bring_in_order(shard, place, pieces, lane, target, sems):
    lanes = slice(lane, lane + target.shape[1])
    return bring(
        [
            (piece.at[here, lanes], target.at[there, :])
            for piece, here, there in places(shard, place, pieces)
        ],
        sems,
    )


def norm(values, gain):
    center = values - jnp.mean(values, axis=-1, keepdims=True)
    spread = jnp.mean(center * center, axis=-1, keepdims=True)
    return center * lax.rsqrt(spread + 1e-05) * gain


def land_start(tokens, mask, embed):
    cols, rows = mask.shape
    total = rows * cols
    row_of = (iota((total, rows), 0) // cols == iota((total, rows), 1)).astype(jnp.bfloat16)
    spread = dot_t(row_of, mask.astype(jnp.bfloat16))
    own = iota((total, cols), 0) % cols == iota((total, cols), 1)
    land = jnp.sum(jnp.where(own, spread, 0.0), axis=1, keepdims=True)
    return tokens.astype(jnp.float32).reshape(total, tokens.shape[2]) + land * embed


def packed_start(packed, embed):
    total = packed.shape[0] - EXTRA
    row = packed[total : total + 1, :total].astype(jnp.float32)
    same = iota((total, total), 0) == iota((total, total), 1)
    land = jnp.sum(jnp.where(same, row, 0.0), axis=1, keepdims=True)
    return packed[:total, :].astype(jnp.float32) + land * embed


def slots(cols, rows, side, inverse=False):
    total = cols * rows
    spot, grid = iota((total, total), int(inverse)), iota((total, total), int(not inverse))
    column = lax.rem(spot // rows + side * (cols // 2), cols)
    return (grid == lax.rem(spot, rows) * cols + column).astype(jnp.bfloat16)


def first_kernel(lons, tokens, mask, project, output, keep, send, packed, *scratch):
    place = own_place()
    *held, sems = scratch
    coming = bring(zip((tokens, mask, project, output), held), sems)
    tokens, mask, project, output = held
    rows, cols, width = tokens.shape
    half = rows * cols // 2
    side = place[0] // (lons // 2)
    to_slots = slots(cols, rows, side)
    wait(coming[:2])
    flat = tokens[...].astype(jnp.float32).reshape(rows * cols, width).astype(jnp.bfloat16)
    in_slots = dot(to_slots, flat).astype(jnp.bfloat16)
    land = mask[...].astype(jnp.float32)
    parts = [land[c : c + 1, :] for c in range(cols)]
    halves = [jnp.concatenate(parts[: cols // 2], axis=1), jnp.concatenate(parts[cols // 2 :], axis=1)]
    for k, out in enumerate((keep, send)):
        out[:half, :] = in_slots[k * half : (k + 1) * half]
        out[half:, :] = jnp.zeros((EXTRA, width), jnp.bfloat16)
        row = jnp.where(side == k, halves[0], halves[1])
        out[half:, :half] = jnp.broadcast_to(row, (EXTRA, half)).astype(jnp.bfloat16)
    wait(coming[2:])
    split = project.shape[1]
    packed[:, :split] = by_kind(project[...])
    packed[:, split:] = output[...]


def column_norm_kernel(own, other, embed, gain, out):
    half = own.shape[0] - EXTRA
    for k, ref in enumerate((own, other)):
        normed = norm(packed_start(ref[...], embed[...]), gain[...])
        out[k * half : (k + 1) * half, :] = normed.astype(jnp.bfloat16)


def unit_heads(vectors, scale=1.0):
    width = vectors.shape[1]
    same = (iota((width, width), 0) // HS == iota((width, width), 1) // HS).astype(jnp.bfloat16)
    total = dot((vectors * vectors).astype(jnp.bfloat16), same)
    return (vectors * (lax.rsqrt(total * (1.0 / HS) + 1e-06) * scale)).astype(jnp.bfloat16)


def two_heads(query, keyed, valued, bias):
    rows = query.shape[0]
    first = iota(query.shape, 1) < HS
    zero = jnp.zeros_like(query)
    stacked = jnp.concatenate([jnp.where(first, query, zero), jnp.where(first, zero, query)], axis=0)
    weight = jnp.exp(dot_t(stacked, keyed) + bias).astype(jnp.bfloat16)
    widened = jnp.concatenate([valued, jnp.ones_like(valued)], axis=1)
    mixed = dot(weight, widened)
    mixed = mixed[:, :PAIR] / mixed[:, PAIR:]
    return jnp.where(first, mixed[:rows], mixed[rows:]).astype(jnp.bfloat16)


def column_kernel(band, slopes, tokens, far_tokens, weight, out_own, out_other, qkv):
    place = own_place()
    block = tokens.shape[0] // 2
    loops = block // band
    width = weight.shape[1] // 3
    for half, ref in enumerate((tokens, far_tokens)):
        projected = dot(ref[...], weight[...])
        at_rows = slice(half * 2 * block, (half + 1) * 2 * block)
        qkv[at_rows, :width] = unit_heads(projected[:, :width], 1.0 / math.sqrt(HS))
        qkv[at_rows, width : 2 * width] = unit_heads(projected[:, width : 2 * width])
        qkv[at_rows, 2 * width :] = projected[:, 2 * width :].astype(jnp.bfloat16)
    total = 2 * band
    shape = (2 * total, 2 * total)
    spot_q, spot_k = iota(shape, 0), iota(shape, 1)
    shift = place[1] * band
    row_q, row_k = lax.rem(spot_q + shift, total), lax.rem(spot_k + shift, total)
    pair_sum = row_q + row_k
    beyond = jnp.minimum(pair_sum + 1, 2 * total - 1 - pair_sum)
    here = (spot_q < total) == (spot_k < total)
    distance = jnp.where(here, jnp.abs(row_q - row_k), beyond).astype(jnp.float32)
    first = place[1] * (width // HS)
    for pair in range(width // PAIR):
        bias = jnp.concatenate(
            [distance * -slopes[first + 2 * pair + one] for one in range(2)], axis=0
        )
        lanes = slice(pair * PAIR, (pair + 1) * PAIR)
        for loop in range(loops):
            starts = [part * block + loop * band for part in range(4)]
            query, keyed, valued = (
                jnp.concatenate(
                    [
                        qkv[at : at + band, kind * width + lanes.start : kind * width + lanes.stop]
                        for at in starts
                    ],
                    axis=0,
                )
                for kind in range(3)
            )
            mixed = two_heads(query, keyed, valued, bias)
            for part in range(4):
                out = (out_own, out_other)[part % 2]
                slot = (part // 2) * loops + loop
                out[slot * band : (slot + 1) * band, lanes] = mixed[part * band : (part + 1) * band]


def middle_kernel(cols, mine, theirs, near, far, kept, got, embed, gain, out):
    update = dot_t(mine[...], near[...]) + dot_t(theirs[...], far[...])
    parts = [packed_start(ref[...], embed[...]) for ref in (kept, got)]
    middle = jnp.concatenate(parts, axis=0) + update
    normed = norm(middle, gain[...]).astype(jnp.bfloat16)
    by_row = slots(cols, normed.shape[0] // cols, 0, True)
    out[...] = dot(by_row, normed).astype(jnp.bfloat16)


def home_kernel(shard, lons, mine, theirs, back, near, far, *refs):
    place = own_place()
    pieces, (tokens, mask, embed, out, out_weight, *held, weight_sems, sems) = refs[:-10], refs[-10:]
    lane = pieces[0].shape[1] - out_weight.shape[2]
    coming = bring(zip((tokens, mask, embed), held), sems)
    count = len(pieces) // 2
    later = []
    for half in range(2):
        mine_of = pieces[half * count : (half + 1) * count]
        later += bring_in_order(shard, place, mine_of, lane, out_weight.at[half], weight_sems.at[half])
    tokens, mask, embed = held
    rows, cols, _ = tokens.shape
    half, width = rows * cols // 2, near.shape[1]
    to_grid = slots(cols, rows, place[0] // (lons // 2), True)
    update = 0.0
    for lane, (kept, weight) in enumerate(((mine, near), (theirs, far))):
        mixed = dot(to_grid[:, :half], kept[:half, :])
        mixed += dot(to_grid[:, half:], back[:, lane * width : (lane + 1) * width])
        update += dot_t(mixed.astype(jnp.bfloat16), weight[...])
    wait(coming)
    out[...] = land_start(tokens[...], mask[...], embed[...]) + update
    wait(later)


def row_kernel(shard, cols, rows, slopes, spread, *refs):
    place = own_place()
    pieces, (out, tokens, weight, sems, token_sem) = refs[:-5], refs[-5:]
    count = len(pieces) // 2
    fetch = lambda half: bring_in_order(
        shard, place, pieces[half * count : (half + 1) * count], 0, weight.at[half], sems.at[half]
    )
    first_copy = bring([(spread, tokens)], token_sem)
    coming = fetch(0)
    total = tokens.shape[0]
    block = cols * rows
    lon_count = total // block
    circle = lon_count * cols
    turn, part = lon_count // 2, cols // 2
    spot_q, spot_k = iota((total, total), 0), iota((total, total), 1)

    def lon_of(spot):
        device, slot = spot // block, lax.rem(spot, cols)
        side = device // turn
        holder = lax.rem(device + (slot // part) * turn, lon_count)
        return holder * cols + side * part + lax.rem(slot, part)

    row_of = lambda spot: lax.rem(spot, block) // cols
    gap = jnp.abs(lon_of(spot_q) - lon_of(spot_k))
    distance = jnp.minimum(gap, circle - gap).astype(jnp.float32)
    column = lax.rem(spot_q, cols)
    away = (column // part != spot_q // block // turn).astype(jnp.int32)
    home = lax.rem(spot_q // block + away * turn, lon_count) * block
    home = home + row_of(spot_q) * cols + away * part + lax.rem(column, part)
    homeward = (spot_k == home).astype(jnp.bfloat16)
    same = row_of(spot_q) == row_of(spot_k)
    width = weight.shape[2] // 3
    heads = width // HS
    wait(first_copy)
    for half in range(2):
        first = lax.rem(place[1] + half, 2) * heads
        wait(coming)
        if half == 0:
            coming = fetch(1)
        projected = dot(tokens[...], weight[half])
        query = unit_heads(projected[:, :width], 1.0 / math.sqrt(HS))
        keyed = unit_heads(projected[:, width : 2 * width])
        valued = projected[:, 2 * width :].astype(jnp.bfloat16)
        mixed = []
        for pair in range(width // PAIR):
            lanes = slice(pair * PAIR, (pair + 1) * PAIR)
            bias = jnp.concatenate(
                [
                    jnp.where(same, distance * -slopes[first + 2 * pair + one], NEVER)
                    for one in range(2)
                ],
                axis=0,
            )
            mixed.append(two_heads(query[:, lanes], keyed[:, lanes], valued[:, lanes], bias))
        mixed = jnp.concatenate(mixed, axis=1)
        out[:, half * width : (half + 1) * width] = dot(homeward, mixed).astype(jnp.bfloat16)


def final_kernel(mixed, middle, weight, out, *refs):
    *held, staged, sems = refs
    mixed_held, weight_held, middle_held = held
    halves = [(weight.at[half], weight_held.at[half]) for half in range(2)]
    coming = bring([(mixed, mixed_held), *halves, (middle, middle_held)], sems)
    mixed, weight, middle = held
    width = weight.shape[2]
    wait(coming[:2])
    update = dot_t(mixed[:, :width], weight[0])
    wait(coming[2:3])
    update += dot_t(mixed[:, width:], weight[1])
    wait(coming[3:])
    staged[...] = (middle[...] + update).reshape(out.shape).astype(jnp.bfloat16)
    wait(bring([(staged, out)], sems))


def fast(
    fields,
    land_mask,
    land_embed,
    column_gain,
    row_gain,
    column_slopes,
    row_slopes,
    column_project,
    column_output,
    row_project,
    row_output,
):
    lon_count = lax.axis_size("lon")
    band, cols, width = fields.shape
    tokens = band * cols
    attend = column_slopes.shape[0] // 2 * HS
    shard = column_project.shape[0]
    embed, column_gain, row_gain = (v.reshape(1, width) for v in (land_embed, column_gain, row_gain))
    mask = land_mask.T
    bf16 = lambda *shape: jax.ShapeDtypeStruct(shape, jnp.bfloat16)
    f32 = lambda *shape: jax.ShapeDtypeStruct(shape, jnp.float32)
    vmem = lambda *arrays: [pltpu.VMEM(v.shape, v.dtype) for v in arrays]
    sems = lambda *shape: [pltpu.SemaphoreType.DMA(shape)]
    after = lax.optimization_barrier
    project_shape = bf16(shard * lon_count, 3 * attend)
    output_shape = bf16(shard * lon_count, attend)
    antipode = lambda value: lax.ppermute(
        value, "lon", at(lambda i: (i + lon_count // 2) % lon_count, lon_count)
    )
    two_lines = lambda value: lax.ppermute(value, "lon", at(lambda i: i ^ (2 * PLANE), lon_count))

    given = (fields, mask, row_project, row_output)
    packed = bf16(tokens // 2 + EXTRA, width)
    keep, send, row_weights = call(
        functools.partial(first_kernel, lon_count),
        (packed, packed, bf16(shard, 4 * attend)),
        "loop_tokens",
        given=given,
        scratch=vmem(*given) + sems(4),
        room=60,
    )
    lines = along_lines(column_project, lon_count)
    output_got, row_got = two_lines(column_output), two_lines(row_weights)
    keep_other = swap_bands(keep)
    *lines, send = after((*lines, send))
    far = antipode(send)
    project = jnp.concatenate([column_project, *lines], axis=0)
    output = jnp.concatenate([column_output, output_got], axis=0)
    row_weights = jnp.concatenate([row_weights, row_got], axis=0)
    project, keep_other = after((project, keep_other))
    project = across_plane(project, lon_count)
    output = doubled(output, PLANE, lon_count)
    far_other = swap_bands(far)

    column_normed = lambda own, other, name: call(
        column_norm_kernel, bf16(tokens, width), name, (own, other, embed, column_gain)
    )
    kept_normed = column_normed(keep, keep_other, "column_normed")
    far_normed = column_normed(far, far_other, "far_normed")
    far_normed, project, output = after((far_normed, project, output))
    project = call(
        functools.partial(order_kernel, shard, True), project_shape, "column_project", project
    )
    row_weights, _ = after((row_weights, far))
    output = across_plane(output, lon_count)
    row_weights = doubled(row_weights, PLANE, lon_count)
    mixed_own, mixed_other = call(
        functools.partial(column_kernel, band),
        (bf16(tokens, attend), bf16(tokens, attend)),
        "column_attention",
        (kept_normed, far_normed, project),
        scalars=(column_slopes,),
        scratch=[pltpu.VMEM((2 * tokens, 3 * attend), jnp.bfloat16)],
        cost=2**18,
    )
    theirs = swap_bands(mixed_other)
    output, row_weights, mixed_own = after((output, row_weights, mixed_own))
    output = call(functools.partial(order_kernel, shard, False), output_shape, "column_output", output)
    output_far = swap_bands(output)

    to_home = jnp.concatenate([mixed_own[tokens // 2 :], theirs[tokens // 2 :]], axis=1)
    row_weights, late = relayed_plane(row_weights, lon_count)
    row_normed = call(
        functools.partial(middle_kernel, cols),
        bf16(tokens, width),
        "row_normed",
        (mixed_own, theirs, output, output_far, keep, far, embed, row_gain),
        cost=2**20,
    )
    spread = lax.all_to_all(row_normed, "lon", split_axis=0, concat_axis=0, tiled=True)
    to_home, row_weights = after((to_home, row_weights))
    home = antipode(to_home)
    row_weights = row_weights + late
    row_weights += [swap_bands(piece) for piece in row_weights]

    row_mixed = call(
        functools.partial(row_kernel, shard, cols, band // lon_count),
        bf16(tokens, 2 * attend),
        "row_attention",
        scalars=(row_slopes,),
        given=(spread, *row_weights),
        scratch=vmem(spread.reshape(tokens, width))
        + [pltpu.VMEM((2, *project_shape.shape), jnp.bfloat16)]
        + sems(2, lon_count)
        + sems(1),
        room=51,
        given_space=pl.ANY,
    )
    row_mixed, home = after((row_mixed, home))
    back = lax.all_to_all(row_mixed, "lon", split_axis=0, concat_axis=0, tiled=True)
    given = (fields, mask, embed)
    middle, row_out = call(
        functools.partial(home_kernel, shard, lon_count),
        (f32(tokens, width), bf16(2, *output_shape.shape)),
        "middle",
        (mixed_own, theirs, home, output, output_far),
        given=(*row_weights, *given),
        scratch=vmem(*given) + sems(2, lon_count) + sems(3),
        room=56,
    )
    return call(
        final_kernel,
        bf16(band, cols, width),
        "block_output",
        given=(back, middle, row_out),
        scratch=vmem(back, row_out, middle) + [pltpu.VMEM(fields.shape, jnp.bfloat16)] + sems(4),
        room=60,
        space=pltpu.HBM,
    )


def passed_along(value, axis, by):
    length = lax.axis_size(axis)
    return lax.ppermute(value, axis, [(i, (i + by) % length) for i in range(length)])


def layer_norm(values, gain):
    center = values - jnp.mean(values, axis=-1, keepdims=True)
    spread = jnp.mean(center * center, axis=-1, keepdims=True)
    return center * lax.rsqrt(spread + 1e-05) * gain


def unit_rms(vectors):
    return vectors * lax.rsqrt(jnp.mean(vectors * vectors, axis=-1, keepdims=True) + 1e-06)


def head_split(projected):
    query = unit_rms(projected[..., 0, :]).astype(jnp.bfloat16)
    keyed = unit_rms(projected[..., 1, :]).astype(jnp.bfloat16)
    valued = projected[..., 2, :].astype(jnp.bfloat16)
    return (query, keyed, valued)


def gather_bands(normed):
    return lax.all_gather(normed, "lat", axis=0, tiled=True)


def sum_heads(partial_value):
    return lax.psum_scatter(
        partial_value.astype(jnp.bfloat16), "lat", scatter_dimension=0, tiled=True
    ).astype(jnp.float32)


def project_in(normed, weight):
    return jnp.dot(
        normed,
        lax.all_gather(weight, "lon", axis=0, tiled=True),
        preferred_element_type=jnp.float32,
    )


def project_out(mixed, weight):
    return lax.dot_general(
        mixed,
        lax.all_gather(weight, "lon", axis=0, tiled=True),
        (((1,), (1,)), ((), ())),
        preferred_element_type=jnp.float32,
    )


def column_attend(query, column_kv, far_kv, slopes):
    total_rows = column_kv.shape[0]
    keyed = jnp.concatenate([column_kv[..., :HS], far_kv[..., :HS]], axis=0)
    valued = jnp.concatenate([column_kv[..., HS:], far_kv[..., HS:]], axis=0)
    scores = jnp.einsum("rchd,schd->chrs", query, keyed, preferred_element_type=jnp.float32)
    rows_here = jnp.arange(query.shape[0], dtype=jnp.int32)
    key_rows = jnp.arange(total_rows, dtype=jnp.int32)
    near_dist = jnp.abs(rows_here[:, None] - key_rows[None, :])
    pair_sum = rows_here[:, None] + key_rows[None, :]
    far_dist = jnp.minimum(pair_sum + 1, 2 * total_rows - 1 - pair_sum)
    distance = jnp.concatenate([near_dist, far_dist], axis=1).astype(jnp.float32)
    weight = jnp.exp(scores * (1.0 / math.sqrt(HS)) - slopes[None, :, None, None] * distance)
    prob = (weight / jnp.sum(weight, axis=-1, keepdims=True)).astype(jnp.bfloat16)
    mixed = jnp.einsum("chrs,schd->rchd", prob, valued, preferred_element_type=jnp.float32)
    return mixed.astype(jnp.bfloat16).reshape(query.shape[0], query.shape[1], -1)


def general(
    fields,
    land_mask,
    land_embed,
    column_gain,
    row_gain,
    column_slopes,
    row_slopes,
    column_project,
    column_output,
    row_project,
    row_output,
):
    lon_count = lax.axis_size("lon")
    lat_count = lax.axis_size("lat")
    band_rows, local_cols, width = fields.shape
    lat_place = lax.axis_index("lat")
    head_total = column_slopes.shape[0]
    head_share = head_total // lat_count
    first_head = lat_place * head_share
    start = fields.astype(jnp.float32) + land_mask.astype(jnp.float32)[..., None] * land_embed
    normed = layer_norm(start, column_gain).astype(jnp.bfloat16)
    whole = gather_bands(normed)
    projected = project_in(whole.reshape(-1, width), column_project)
    query, keyed, valued = head_split(
        projected.reshape(band_rows * lat_count, local_cols, head_share, 3, HS)
    )
    column_kv = jnp.concatenate([keyed, valued], axis=-1).reshape(
        band_rows * lat_count, local_cols, -1
    )
    slopes = lax.dynamic_slice_in_dim(column_slopes, first_head, head_share)
    far_kv = passed_along(column_kv, "lon", lon_count // 2)
    shaped = column_kv.shape[:2] + (head_share, 2 * HS)
    mixed = column_attend(query, column_kv.reshape(shaped), far_kv.reshape(shaped), slopes)
    partial_value = project_out(mixed.reshape(-1, head_share * HS), column_output)
    update = sum_heads(partial_value.reshape(band_rows * lat_count, local_cols, width))
    middle = start + update
    total_rows = band_rows * lat_count
    row_normed = layer_norm(middle, row_gain).astype(jnp.bfloat16)
    whole_rows = gather_bands(row_normed)
    projected = project_in(whole_rows.reshape(-1, width), row_project)
    query, keyed, valued = head_split(projected.reshape(total_rows, local_cols, head_share, 3, HS))
    packed = jnp.stack([query, keyed, valued], axis=3)
    parts = lax.all_to_all(packed, "lon", split_axis=0, concat_axis=1, tiled=True)
    few_rows, all_cols = (parts.shape[0], parts.shape[1])
    scores = jnp.einsum(
        "rchd,rehd->rhce", parts[..., 0, :], parts[..., 1, :], preferred_element_type=jnp.float32
    )
    cols_here = jnp.arange(all_cols, dtype=jnp.int32)
    gap = jnp.abs(cols_here[:, None] - cols_here[None, :])
    cycle_dist = jnp.minimum(gap, all_cols - gap).astype(jnp.float32)
    row_slope = lax.dynamic_slice_in_dim(row_slopes, first_head, head_share)
    weight = jnp.exp(scores * (1.0 / math.sqrt(HS)) - row_slope[None, :, None, None] * cycle_dist)
    prob = (weight / jnp.sum(weight, axis=-1, keepdims=True)).astype(jnp.bfloat16)
    row_mixed = jnp.einsum(
        "rhce,rehd->rchd", prob, parts[..., 2, :], preferred_element_type=jnp.float32
    )
    row_mixed = row_mixed.astype(jnp.bfloat16)
    back = lax.all_to_all(row_mixed, "lon", split_axis=1, concat_axis=0, tiled=True)
    partial_value = project_out(back.reshape(-1, head_share * HS), row_output)
    final_update = sum_heads(partial_value.reshape(total_rows, local_cols, width))
    return (middle + final_update).astype(jnp.bfloat16)


def solution(mesh):
    in_specs = (
        P("lat", "lon", None),
        P("lat", "lon"),
        P(),
        P(),
        P(),
        P(),
        P(),
        P("lon", "lat"),
        P("lon", "lat"),
        P("lon", "lat"),
        P("lon", "lat"),
    )
    out_specs = P(("ens", "lat"), "lon", None)

    def shards(fields, *rest):
        length = lax.axis_size("lon")
        suits = fields.shape[0] % length == 0 and length == 4 * PLANE
        return (fast if suits else general)(fields, *rest)

    return jax.shard_map(shards, mesh=mesh, in_specs=in_specs, out_specs=out_specs, check_vma=False)
```
